512 devices in a mesh: dp: 128 (over z, x, y_hi), rep: 4 (over y_lo, core).
Axes of the slice: x: 4, y: 8 (y_hi: 4, y_lo: 2; y = y_hi * 2 + y_lo), z: 8, core: 2. Of those that a mesh axis runs over, the one named last changes fastest.
Arguments:
- projections: float32 [32768, 256], P('dp'), may hold values from -7 to 7
- partner: int32 [32768], P('dp'), may hold values from 0 to 32767, as said below
- cotangent: float32 [32768], P('dp'), may hold values from 0.3 to 3
Outputs:
- row_loss: float32 [32768], P('dp')
- grad_projections: float32 [32768, 256], P('dp')
The draws below stay inside these ranges and needn't reach their ends.
Inputs may be any that keep to these rules, and one draw needn't show every extreme that they name: partner[partner[i]] = i and partner[i] != i for every view i.
All inputs are finite; a program needn't handle non-finite values.
Results may differ from the reference program's by a relative error of at most 0.0003.
Values sent between devices are 32-bit elements; how exact they have to be, the bound alone decides.
No kernel may reach another device: no remote copies, remote signals or barrier semaphores. Data moves between devices by JAX's collectives and lax.ppermute only.
A program may use at most 64 MiB of HBM per device.

```python
import math
import jax
import jax.numpy as jnp
from jax import lax

ROWS_DEV = 256
D = 256
VIEWS = 32768


def pairing(key):
    return jax.random.permutation(key, VIEWS).astype(jnp.int32)


def draw_partner(key, part):
    shuffled = pairing(key)
    first_views = shuffled[0::2]
    second_views = shuffled[1::2]
    matched = jnp.zeros((VIEWS,), jnp.int32).at[first_views].set(second_views)
    return matched.at[second_views].set(first_views)


def draw_projections(key, part):
    shuffled = pairing(key)
    key = jax.random.fold_in(key, 23)
    key_base, key_noise = jax.random.split(key, 2)
    slot_of = jnp.zeros((VIEWS,), jnp.int32).at[shuffled].set(jnp.arange(VIEWS, dtype=jnp.int32))
    pair_index = slot_of // 2
    image_part = jax.random.normal(key_base, (VIEWS // 2, D), jnp.float32)
    view_noise = 0.7 * jax.random.normal(key_noise, (VIEWS, D), jnp.float32)
    values = image_part[pair_index] + view_noise
    return jnp.clip(values, -7.0, 7.0).astype(jnp.float32)


def block_scale(rng, dims, cuts, least, high):
    loudness = 1.0
    for dim, parts in cuts:
        steps = jax.random.uniform(jax.random.fold_in(jax.random.fold_in(rng, 6), dim), (parts,), jnp.float32, least / len(cuts), high / len(cuts))
        loudness = loudness * jnp.repeat(jnp.exp(steps), dims[dim] // parts).reshape((-1,) + (1,) * (len(dims) - 1 - dim))
    return loudness


def setup_inputs(seed: int = 0) -> dict:
    key_of = jax.random.split(jax.random.key(seed), 4)
    return {
        "projections": draw_projections(jax.random.fold_in(key_of[3], 71), 0),
        "partner": draw_partner(jax.random.fold_in(key_of[3], 71), 0),
        "cotangent": jnp.clip(jnp.exp(math.log(3.0) - 2.3025851 * jax.random.uniform(key_of[2], (VIEWS,), jnp.float32) ** block_scale(key_of[2], (VIEWS,), ((0, 128),), -0.2, 0.2)), 0.3, 3.0),
    }


inv_temp = 10.0
epsilon = 1e-06
highest = lax.Precision.HIGHEST

def reference(projections, partner, cotangent):
    row_norms = jnp.sqrt(lax.optimization_barrier(jnp.sum(projections * projections, axis=1)) + epsilon)
    unit_rows = projections / row_norms[:, None]
    view_count = unit_rows.shape[0]
    all_ids = jnp.arange(view_count, dtype=jnp.int32)
    block_total = view_count // ROWS_DEV

    def block_parts(block_index):
        row_start = (block_index * ROWS_DEV).astype(jnp.int32)
        rows_here = lax.dynamic_slice_in_dim(unit_rows, row_start, ROWS_DEV, 0)
        ids_here = row_start + jnp.arange(ROWS_DEV, dtype=jnp.int32)
        partner_here = lax.dynamic_slice_in_dim(partner, row_start, ROWS_DEV, 0)
        scores = inv_temp * jnp.dot(rows_here, unit_rows.T, precision=highest, preferred_element_type=jnp.float32)
        notself = (ids_here[:, None] != all_ids[None, :]).astype(jnp.float32)
        paired = (partner_here[:, None] == all_ids[None, :]).astype(jnp.float32)
        return (row_start, scores, notself, paired)

    def first_pass(block_index):
        row_start, scores, notself, paired = block_parts(block_index)
        exp_sums = lax.optimization_barrier(jnp.sum(jnp.exp(scores) * notself, axis=1))
        positive = lax.optimization_barrier(jnp.sum(scores * paired, axis=1))
        return (exp_sums, positive)
    blocks = jnp.arange(block_total, dtype=jnp.int32)
    exp_sums, positive = lax.map(first_pass, blocks)
    exp_sums = exp_sums.reshape(view_count)
    positive = positive.reshape(view_count)
    log_sums = jnp.log(exp_sums)
    row_loss = log_sums - positive

    def second_pass(block_index):
        row_start, scores, notself, paired = block_parts(block_index)
        own_logs = lax.dynamic_slice_in_dim(log_sums, row_start, ROWS_DEV, 0)
        own_weight = lax.dynamic_slice_in_dim(cotangent, row_start, ROWS_DEV, 0)
        own_part = jnp.exp(scores - own_logs[:, None]) * notself
        seen_part = jnp.exp(scores - log_sums[None, :]) * notself
        pair_weights = own_weight[:, None] * (own_part - paired) + cotangent[None, :] * (seen_part - paired)
        return jnp.dot(pair_weights, unit_rows, precision=highest, preferred_element_type=jnp.float32)
    unit_grad = inv_temp * lax.map(second_pass, blocks).reshape(view_count, unit_rows.shape[1])
    along = lax.optimization_barrier(jnp.sum(unit_rows * unit_grad, axis=1))
    grad_projections = (unit_grad - unit_rows * along[:, None]) / row_norms[:, None]
    return (row_loss, grad_projections)
```

```python
import functools

import jax
import jax.numpy as jnp
from jax import lax
from jax.experimental import pallas as pl
from jax.experimental.pallas import tpu as pltpu
from jax.sharding import Mesh, PartitionSpec as P

inv_temp = 10.0
epsilon = 1e-06
tile = 256
group = ("yh", "yl", "core")
sizes = {"z": 8, "x": 4, "yh": 4, "yl": 2, "core": 2}
mib = 1024 * 1024


def halves(array):
    high = array.astype(jnp.bfloat16)
    low = (array - high.astype(jnp.float32)).astype(jnp.bfloat16)
    return high, low


def as_column(row):
    return jnp.transpose(jnp.broadcast_to(row, (128, row.shape[1])))[:, 0:1]


def as_row(column):
    return jnp.transpose(jnp.broadcast_to(column, (column.shape[0], 128)))[0:1, :]


def column_ids(first, count):
    place = lax.broadcasted_iota(jnp.int32, (1, count), 1)
    return first + (place >> 6) * 1024 + (place & 63)


def score_kernel(firsts, rows, cols, partner, exps, sums, col_high, col_low):
    step = pl.program_id(0)

    @pl.when(step == 0)
    def _():
        high, low = halves(cols[...])
        col_high[...] = high
        col_low[...] = low

    row_high, row_low = halves(rows[...] * inv_temp)
    nt = functools.partial(
        lax.dot_general,
        dimension_numbers=(((1,), (1,)), ((), ())),
        preferred_element_type=jnp.float32,
    )
    scores = (
        nt(row_high, col_high[...]) + nt(row_high, col_low[...]) + nt(row_low, col_high[...])
    )
    ids = column_ids(firsts[1], cols.shape[0])
    row_ids = firsts[0] + step * tile + lax.broadcasted_iota(jnp.int32, (tile, 1), 0)
    exp_scores = jnp.where(row_ids == ids, 0.0, jnp.exp(scores))
    exps[...] = exp_scores
    hits = jnp.where(as_column(partner[...]) == ids, scores, 0.0)
    sums[0:1, :] = as_row(jnp.sum(exp_scores, axis=1, keepdims=True))
    sums[1:2, :] = as_row(jnp.sum(hits, axis=1, keepdims=True))


def grad_kernel(firsts, exps, cols, partner, own, seen, out, col_high, col_low):
    step = pl.program_id(0)

    @pl.when(step == 0)
    def _():
        high, low = halves(cols[...])
        col_high[...] = high
        col_low[...] = low

    ids = column_ids(firsts[1], cols.shape[0])
    paired = as_column(partner[...]) == ids
    own_scale, own_weight = as_column(own[0:1, :]), as_column(own[1:2, :])
    weights = exps[...] * (own_scale + seen[0:1, :]) - jnp.where(
        paired, own_weight + seen[1:2, :], 0.0
    )
    high, low = halves(weights)
    nn = functools.partial(jnp.dot, preferred_element_type=jnp.float32)
    sums = nn(high, col_high[...]) + nn(high, col_low[...]) + nn(low, col_high[...])
    for part in range(4):
        out[part % 2, 0, part // 2] = sums[part * 64 : (part + 1) * 64]


def scores_of(firsts, rows, cols, partner):
    count, width = rows.shape
    seen = cols.shape[0]
    return pl.pallas_call(
        score_kernel,
        grid=(count // tile,),
        in_specs=[
            pl.BlockSpec(memory_space=pltpu.SMEM),
            pl.BlockSpec((tile, width), lambda i: (i, 0)),
            pl.BlockSpec((seen, width), lambda i: (0, 0)),
            pl.BlockSpec((1, tile), lambda i: (0, i)),
        ],
        out_specs=[
            pl.BlockSpec((tile, seen), lambda i: (i, 0)),
            pl.BlockSpec((2, tile), lambda i: (0, i)),
        ],
        out_shape=[
            jax.ShapeDtypeStruct((count, seen), jnp.float32),
            jax.ShapeDtypeStruct((2, count), jnp.float32),
        ],
        scratch_shapes=[pltpu.VMEM((seen, width), jnp.bfloat16)] * 2,
        compiler_params=pltpu.CompilerParams(vmem_limit_bytes=40 * mib),
        cost_estimate=pl.CostEstimate(
            flops=6 * count * seen * width,
            bytes_accessed=4 * (count * seen + (count + seen) * width),
            transcendentals=count * seen,
        ),
    )(firsts, rows, cols, partner)


def grads_of(firsts, exps, cols, partner, own, seen):
    count, seen_count = exps.shape
    width = cols.shape[1]
    return pl.pallas_call(
        grad_kernel,
        grid=(count // tile,),
        in_specs=[
            pl.BlockSpec(memory_space=pltpu.SMEM),
            pl.BlockSpec((tile, seen_count), lambda i: (i, 0)),
            pl.BlockSpec((seen_count, width), lambda i: (0, 0)),
            pl.BlockSpec((1, tile), lambda i: (0, i)),
            pl.BlockSpec((2, tile), lambda i: (0, i)),
            pl.BlockSpec((2, seen_count), lambda i: (0, 0)),
        ],
        out_specs=pl.BlockSpec((2, 1, 2, 64, width), lambda i: (0, i, 0, 0, 0)),
        out_shape=jax.ShapeDtypeStruct((2, count // tile, 2, 64, width), jnp.float32),
        scratch_shapes=[pltpu.VMEM((seen_count, width), jnp.bfloat16)] * 2,
        compiler_params=pltpu.CompilerParams(vmem_limit_bytes=40 * mib),
        cost_estimate=pl.CostEstimate(
            flops=6 * count * seen_count * width,
            bytes_accessed=4 * (count * seen_count + (count + seen_count) * width),
            transcendentals=0,
        ),
    )(firsts, exps, cols, partner, own, seen)


def told_all(part, axes, count):
    return lax.all_to_all(jnp.broadcast_to(part[None], (count,) + part.shape), axes, 0, 0, tiled=True)


def per_device(projections, partner, cotangent):
    at = {name: lax.axis_index(name) for name in sizes}
    member = at["yl"] * 2 + at["core"]
    row_norms = jnp.sqrt(jnp.sum(projections * projections, axis=1, keepdims=True) + epsilon)
    unit = projections / row_norms
    quarter = lax.dynamic_slice_in_dim(unit, member * 64, 64, 0)
    cols = lax.all_gather(lax.all_gather(quarter, "x", tiled=True), "z", tiled=True)
    rows = lax.all_gather(unit, "yh", tiled=True)
    partner_rows = lax.all_gather(partner, "yh", tiled=True)
    weight_rows = lax.all_gather(cotangent, "yh", tiled=True)
    firsts = jnp.stack([(at["z"] * 4 + at["x"]) * 1024, at["yh"] * 256 + member * 64])
    exps, part_sums = scores_of(firsts, rows, cols, partner_rows[None])
    sums = jnp.sum(told_all(part_sums, group, 16), axis=0)
    losses = jnp.log(sums[0]) - sums[1]
    row_loss = lax.dynamic_slice_in_dim(losses, at["yh"] * 256, 256, 0)
    own = jnp.stack([weight_rows / sums[0], weight_rows])
    own_part = lax.dynamic_slice_in_dim(own, at["yh"] * 256 + member * 64, 64, 1)
    seen = jnp.swapaxes(told_all(own_part, ("z", "x"), 32), 0, 1).reshape(2, -1)
    partial = grads_of(firsts, exps, cols, partner_rows[None], own, seen)
    halved = jnp.sum(lax.all_to_all(partial, "core", 0, 0, tiled=True), axis=0)
    swapped = lax.all_to_all(halved.reshape(8, 64, 256), ("yh", "yl"), 0, 0, tiled=True)
    grad_quarter = inv_temp * jnp.sum(swapped, axis=0)
    norm_quarter = lax.dynamic_slice_in_dim(row_norms, member * 64, 64, 0)
    along = jnp.sum(quarter * grad_quarter, axis=1, keepdims=True)
    grad_quarter = (grad_quarter - quarter * along) / norm_quarter
    return row_loss, lax.all_gather(grad_quarter, ("yl", "core"), tiled=True)


def solution(mesh):
    fine = Mesh(mesh.devices.reshape(tuple(sizes.values())), tuple(sizes))
    blocks = ("z", "x", "yh")
    return jax.shard_map(
        per_device,
        mesh=fine,
        in_specs=(P(blocks, None), P(blocks), P(blocks)),
        out_specs=(P(blocks), P(blocks, None)),
        check_vma=False,
    )
```

```python
import math

import jax
import jax.numpy as jnp
from jax import lax
from jax.experimental import pallas as pl
from jax.experimental.pallas import tpu as pltpu
from jax.sharding import Mesh, PartitionSpec as P

inv_temp = 10.0
epsilon = 1e-06
tile = 256
lanes = 128
quarter = 64
packed = 264
group = ("yh", "yl", "core")
sizes = {"z": 8, "x": 4, "yh": 4, "yl": 2, "core": 2}
steps = (0, 3, 1, 2)
mib = 1024 * 1024
f32, bf16 = jnp.float32, jnp.bfloat16


def halves(array):
    high = array.astype(bf16)
    low = (array - high.astype(f32)).astype(bf16)
    return high, low


def as_column(row):
    return jnp.transpose(jnp.broadcast_to(row, (lanes, row.shape[1])))


def dot(left, right, dims=((1,), (0,))):
    return lax.dot_general(left, right, (dims, ((), ())), preferred_element_type=f32)


def products(left, right, dims=((1,), (0,))):
    return dot(left[0], right[0], dims) + dot(left[0], right[1], dims) + dot(left[1], right[0], dims)


def pieces(array):
    return [array[:, at : at + lanes] for at in range(0, array.shape[1], lanes)]


def fetch(sems, *pairs):
    copies = [pltpu.make_async_copy(a, b, sems.at[i]) for i, (a, b) in enumerate(pairs)]
    for copy in copies:
        copy.start()
    return copies


def wait_all(copies):
    for copy in copies:
        copy.wait()


def blocks_of(ref):
    return [ref.at[pl.ds(at, tile), :] for at in range(0, ref.shape[0], tile)]


def info_pairs(rows, info):
    return [(rows.at[block, pl.ds(tile, 8), :], info.at[block]) for block in range(rows.shape[0])]


def member():
    return lax.axis_index("yl") * 2 + lax.axis_index("core")


def source_of(chunk):
    return lax.rem(lax.axis_index("x") + steps[chunk], 4)


def seen_ids(chunk, count):
    first = source_of(chunk) * 1024 + lax.axis_index("yh") * 256 + member() * quarter
    place = lax.broadcasted_iota(jnp.int32, (1, count), 1)
    return first + (place >> 6) * 4096 + (place & 63)


def start_kernel(
    rows, partner, cotangent, packed_rows, told, unit, norms, partner_in, cotangent_in, packed_in,
    sems,
):
    copies = fetch(
        sems,
        (rows, packed_in.at[pl.ds(0, tile), :]),
        (partner, partner_in),
        (cotangent, cotangent_in),
    )
    packed_in[tile:, :] = jnp.zeros((packed - tile, rows.shape[1]), f32)
    wait_all(copies)
    packed_in[tile : tile + 1, :] = partner_in[...].astype(f32)
    packed_in[tile + 1 : tile + 2, :] = cotangent_in[...]
    copies = fetch(sems, (packed_in, packed_rows))
    own = packed_in[pl.ds(pl.multiple_of(member() * quarter, quarter), quarter), :]
    own_norms = jnp.sqrt(jnp.sum(own * own, axis=1, keepdims=True) + epsilon)
    own_unit = own / own_norms
    unit[...] = own_unit
    norms[...] = jnp.broadcast_to(own_norms, norms.shape)
    told[...] = jnp.broadcast_to(own_unit[None], told.shape)
    wait_all(copies)


def rows_kernel(rows, high, low, partner):
    for block in range(rows.shape[0]):
        at = slice(block * tile, (block + 1) * tile)
        raw = rows[block, :tile, :]
        norms = jnp.sqrt(jnp.sum(raw * raw, axis=1, keepdims=True) + epsilon)
        high[at, :], low[at, :] = halves(raw / norms * (inv_temp * math.log2(math.e)))
        partner[at, :] = as_column(rows[block, tile : tile + 1, :]).astype(jnp.int32)


def score(chunk, at, row_high, row_low, cols, partner, count):
    scores = products((row_high[at, :], row_low[at, :]), cols, ((1,), (1,)))
    ids = seen_ids(chunk, count)
    exps = jnp.exp2(scores)
    if chunk == 0:
        first = (lax.axis_index("z") * 4 + lax.axis_index("x")) * 1024 + at.start
        row_ids = first + lax.broadcasted_iota(jnp.int32, (tile, 1), 0)
        exps = jnp.where(row_ids == ids, 0.0, exps)
    paired = [partner[at, :] == piece for piece in pieces(ids)]
    hits = [jnp.where(p, s, 0.0) for p, s in zip(paired, pieces(scores))]
    return exps, paired, jnp.sum(exps, axis=0, keepdims=True), sum(hits[1:], hits[0])


def paired_sum_of(paired, cols):
    ones = jnp.concatenate([p.astype(f32).astype(bf16) for p in paired], axis=1)
    return dot(ones, cols[0]) + dot(ones, cols[1])


def chunk_kernel(chunk, row_high, row_low, cols, partner, *refs):
    before, refs = refs[: 3 if chunk else 0], refs[3 if chunk else 0 :]
    high_out, low_out, col_sums, hits, plain, paired_rows, high, low, sems = refs
    count = cols.shape[0]
    parts = halves(cols[...])
    copies, totals = [], None
    for block in range(row_high.shape[0] // tile):
        at = slice(block * tile, (block + 1) * tile)
        exps, paired, total, hit = score(chunk, at, row_high, row_low, parts, partner, count)
        totals = total if totals is None else totals + total
        high[at, :], low[at, :] = exp_parts = halves(exps)
        rows_at = pl.ds(at.start, tile)
        copies += fetch(
            sems.at[block],
            (high.at[rows_at, :], high_out.at[rows_at, :]),
            (low.at[rows_at, :], low_out.at[rows_at, :]),
        )
        sums = (hit, products(exp_parts, parts), paired_sum_of(paired, parts))
        for i, (ref, value) in enumerate(zip((hits, plain, paired_rows), sums)):
            ref[at, :] = value + before[i][at, :] if chunk else value
    for part, piece in enumerate(pieces(totals)):
        col_sums[part : part + 1, :] = piece
    wait_all(copies)


def last_kernel(
    row_high, row_low, cols, partner, hits, plain, cotangent, sums_0, sums_1, sums_2, high_out,
    low_out, told, shared, high, low, sums, sems,
):
    count = cols.shape[0]
    parts = halves(cols[...])
    copies, totals = [], None
    for block in range(row_high.shape[0] // tile):
        at = slice(block * tile, (block + 1) * tile)
        exps, _, total, hit = score(3, at, row_high, row_low, parts, partner, count)
        totals = total if totals is None else totals + total
        high[at, :], low[at, :] = exp_parts = halves(exps)
        rows_at = pl.ds(at.start, tile)
        copies += fetch(
            sems.at[block],
            (high.at[rows_at, :], high_out.at[rows_at, :]),
            (low.at[rows_at, :], low_out.at[rows_at, :]),
        )
        summed = products(exp_parts, parts) + plain[at, :]
        hit += hits[at, :]
        for part in range(tile // lanes):
            turned = jnp.transpose(hit[part * lanes : (part + 1) * lanes, :])
            row = math.log(2.0) * jnp.sum(turned, axis=0, keepdims=True)
            for side in range(2):
                k = block * 4 + part * 2 + side
                shared[k, :quarter, :] = summed[(part * 2 + side) * 64 : (part * 2 + side + 1) * 64]
                shared[k, quarter:, :] = jnp.zeros((8, shared.shape[2]), f32)
                here = row if side == 0 else pltpu.roll(row, 64, 1)
                shared[k, quarter : quarter + 1, :lanes] = here
    own = cotangent[pl.ds(lax.axis_index("yl"), 1), :]
    own = jnp.where(lax.axis_index("core") == 0, own, pltpu.roll(own, 64, 1))
    last = jnp.concatenate(pieces(totals), axis=0)
    for chunk, values in enumerate((sums_0[...], sums_1[...], sums_2[...], last)):
        for part in range(4):
            sums[pl.ds(source_of(chunk) * 4 + part, 1), :] = values[part : part + 1, :]
    sums[16:17, :] = own
    sums[17:, :] = jnp.zeros((7, lanes), f32)
    told[...] = jnp.broadcast_to(sums[...][None], told.shape)
    wait_all(copies)


def shadow_kernel(cols, rows, before, out, cols_in, info, paired_rows, sems):
    copies = fetch(sems, (cols, cols_in), (before, paired_rows), *info_pairs(rows, info))
    wait_all(copies)
    parts = halves(cols_in[...])
    ids = pieces(seen_ids(3, cols_in.shape[0]))
    for block in range(paired_rows.shape[0] // tile):
        at = slice(block * tile, (block + 1) * tile)
        partner = as_column(info[block, 0:1, :]).astype(jnp.int32)
        paired_rows[at, :] += paired_sum_of([partner == piece for piece in ids], parts)
    wait_all(fetch(sems, (paired_rows, out)))


def grad_kernel(message, *refs):
    ins, (out, own_sum, *refs) = refs[:14], refs[14:]
    exps, cols, (paired_rows, rows) = ins[:8], ins[8:12], ins[12:]
    exps_in, refs = refs[:8], refs[8:]
    cols_in, paired_in, info, scales, weights, au_high, au_low, total, sems = refs
    arrivals = []
    for chunk in range(4):
        pairs = [(ref, exps_in[i]) for i, ref in enumerate(exps) if i % 4 == chunk]
        arrivals.append(fetch(sems.at[chunk], (cols[chunk], cols_in.at[chunk]), *pairs))
    last = fetch(sems.at[4], (paired_rows, paired_in), *info_pairs(rows, info))
    scales[...] = jnp.sum(message[...], axis=0)[:16, :]
    sums = []
    place = lax.broadcasted_iota(jnp.int32, (1, lanes), 1)
    for chunk in range(4):
        source = source_of(chunk)
        for z in range(0, 8, 2):
            even, odd = (message[(z + side) * 4 + source, 16:17, :] for side in range(2))
            row = chunk * 4 + z // 2
            sums.append(scales[pl.ds(source * 4 + z // 2, 1), :])
            weights[row : row + 1, :] = jnp.where(place < 64, even, pltpu.roll(odd, 64, 1))
    z = lax.axis_index("z")
    own = scales[pl.ds(lax.axis_index("x") * 4 + z // 2, 1), :]
    own_sum[...] = jnp.where(lax.rem(z, 2) == 0, own, pltpu.roll(own, 64, 1))
    columns = jnp.transpose(jnp.concatenate([weights[...] / jnp.concatenate(sums, axis=0)] * 8, axis=0))
    count = cols_in.shape[1]
    ids = []
    for chunk, arrival in enumerate(arrivals):
        arrival[0].wait()
        for part in range(4):
            scaled = cols_in[chunk, part * lanes : (part + 1) * lanes, :]
            scaled *= columns[:, chunk * 4 + part : chunk * 4 + part + 1]
            at = slice(chunk * count + part * lanes, chunk * count + (part + 1) * lanes)
            au_high[at, :], au_low[at, :] = halves(scaled)
        at = slice(chunk * count, (chunk + 1) * count)
        scaled_cols = (au_high[at, :], au_low[at, :])
        ids += pieces(seen_ids(chunk, count))
        wait_all(arrival[1:])
        for block in range(4):
            rows_at = slice(block * tile, (block + 1) * tile)
            added = products(
                (exps_in[chunk][rows_at, :], exps_in[4 + chunk][rows_at, :]), scaled_cols
            )
            total[rows_at, :] = added if chunk == 0 else total[rows_at, :] + added
    wait_all(last)
    for block in range(4):
        rows_at = slice(block * tile, (block + 1) * tile)
        partner = as_column(info[block, 0:1, :]).astype(jnp.int32)
        spread = jnp.zeros((tile, lanes), f32)
        for i, piece in enumerate(ids):
            spread += jnp.where(partner == piece, weights[i : i + 1, :], 0.0)
        weight = as_column(info[block, 1:2, :])[:, :1] + jnp.sum(spread, axis=1, keepdims=True)
        result = total[rows_at, :] - weight * paired_in[rows_at, :]
        for part in range(4):
            out[part % 2, block, part // 2] = result[part * 64 : (part + 1) * 64]


def final_kernel(parts, shared, own_sum, cotangent, unit, norms, out):
    own = cotangent[pl.ds(lax.axis_index("yl"), 1), :]
    own = jnp.where(lax.axis_index("core") == 0, own, pltpu.roll(own, 64, 1))
    scale = as_column(own / own_sum[...])[:quarter, :1]
    grad = inv_temp * (jnp.sum(parts[...], axis=0) + scale * shared[:quarter, :])
    along = jnp.sum(unit[...] * grad, axis=1, keepdims=True)
    out[:quarter, :] = (grad - unit[...] * along) / norms[:, :1]
    out[quarter:, :] = jnp.zeros((8, out.shape[1]), f32)
    out[quarter : quarter + 1, :lanes] = jnp.log(own_sum[...]) - shared[quarter : quarter + 1, :lanes]


vmem, anywhere = pl.BlockSpec(memory_space=pltpu.VMEM), pl.BlockSpec(memory_space=pl.ANY)


def call(kernel, outs, args, limit, cost=None, scratch=(), far=(), far_outs=()):
    args = [
        pltpu.with_memory_space_constraint(arg, pltpu.HBM) if i in far else arg
        for i, arg in enumerate(args)
    ]
    return pl.pallas_call(
        kernel,
        in_specs=[anywhere if i in far else vmem for i in range(len(args))],
        out_specs=[anywhere if i in far_outs else vmem for i in range(len(outs))],
        out_shape=[
            pltpu.HBM(*out) if i in far_outs else jax.ShapeDtypeStruct(*out)
            for i, out in enumerate(outs)
        ],
        scratch_shapes=list(scratch),
        compiler_params=pltpu.CompilerParams(vmem_limit_bytes=limit * mib),
        cost_estimate=cost,
    )(*args)


def estimate(passes, count, seen, width, exps=0):
    return pl.CostEstimate(
        flops=passes * 2 * count * seen * width,
        bytes_accessed=4 * (count * seen + (count + seen) * width),
        transcendentals=exps,
    )


def passed_along(array, by):
    return lax.ppermute(array, "x", [(i, (i + by) % 4) for i in range(4)])


def per_device(projections, partner, cotangent):
    width = projections.shape[1]
    count, seen = 4 * tile, 8 * quarter
    copies = pltpu.SemaphoreType.DMA
    info = pltpu.VMEM((4, 8, width), f32)
    packed_rows, told, own_unit, norms = call(
        start_kernel,
        [((packed, width), f32), ((8, quarter, width), f32), ((quarter, width), f32),
         ((quarter, lanes), f32)],
        (projections, partner[None], cotangent[None]),
        4,
        scratch=[pltpu.VMEM((1, tile), jnp.int32), pltpu.VMEM((1, tile), f32),
                 pltpu.VMEM((packed, width), f32), copies((3,))],
        far=(0, 1, 2),
        far_outs=(0,),
    )
    here = lax.all_to_all(told, "z", 0, 0, tiled=True).reshape(seen, width)
    rows = lax.all_gather(packed_rows, "yh")
    cols = [here, passed_along(here, 1), passed_along(here, -1), passed_along(here, 2)]
    row_high, row_low, partners = call(
        rows_kernel,
        [((count, width), bf16)] * 2 + [((count, lanes), jnp.int32)],
        (rows,),
        8,
    )
    exps_out = [((count, seen), bf16)] * 2
    row_sums = [((count, width), f32)] * 2
    own_exps = [pltpu.VMEM(*out) for out in exps_out]
    own_rows = [pltpu.VMEM(*out) for out in row_sums]
    highs, lows, col_sums, before = [], [], [], ()
    for chunk in range(3):

        def kernel(*refs, chunk=chunk):
            chunk_kernel(chunk, *refs)

        high, low, sums, *before = call(
            kernel,
            exps_out + [((seen // lanes, lanes), f32), ((count, lanes), f32)] + row_sums,
            (row_high, row_low, cols[chunk], partners, *before),
            24,
            estimate(8, count, seen, width, count * seen),
            own_exps + [copies((4, 2))],
            far_outs=(0, 1),
        )
        highs.append(high)
        lows.append(low)
        col_sums.append(sums)
    hits, plain, paired_rows = before
    high, low, told, shared = call(
        last_kernel,
        exps_out + [((32, 24, lanes), f32), ((16, quarter + 8, width), f32)],
        (row_high, row_low, cols[3], partners, hits, plain, cotangent.reshape(2, lanes), *col_sums),
        24,
        estimate(6, count, seen, width, count * seen),
        own_exps + [pltpu.VMEM((24, lanes), f32), copies((4, 2))],
        far_outs=(0, 1),
    )
    highs.append(high)
    lows.append(low)
    shared = lax.psum_scatter(shared.reshape(-1, width), group, tiled=True)
    message = lax.all_to_all(told, ("z", "x"), 0, 0, tiled=True)
    (paired_rows,) = call(
        shadow_kernel,
        row_sums[:1],
        (cols[3], rows, paired_rows),
        16,
        estimate(2, count, seen, width),
        [pltpu.VMEM((seen, width), f32), info, own_rows[0], copies((6,))],
        far=range(3),
        far_outs=(0,),
    )
    partial, own_sum = call(
        grad_kernel,
        [((2, 4, 2, quarter, width), f32), ((1, lanes), f32)],
        (message, *highs, *lows, *cols, paired_rows, rows),
        28,
        estimate(3, count, 4 * seen, width),
        own_exps * 4
        + [pltpu.VMEM((4, seen, width), f32), own_rows[0], info]
        + [pltpu.VMEM((16, lanes), f32)] * 2
        + [pltpu.VMEM((4 * seen, width), bf16)] * 2
        + [own_rows[0], copies((5, 5))],
        far=range(1, 15),
    )
    halved = jnp.sum(lax.all_to_all(partial, "core", 0, 0, tiled=True), axis=0)
    swapped = lax.all_to_all(halved.reshape(8, quarter, width), ("yh", "yl"), 0, 0, tiled=True)
    (result,) = call(
        final_kernel,
        [((quarter + 8, width), f32)],
        (swapped, shared, own_sum, cotangent.reshape(2, lanes), own_unit, norms),
        4,
    )
    result = lax.all_gather(result, ("yl", "core"))
    return result[:, quarter, :quarter].reshape(-1), result[:, :quarter].reshape(-1, width)


def solution(mesh):
    fine = Mesh(mesh.devices.reshape(tuple(sizes.values())), tuple(sizes))
    blocks = ("z", "x", "yh")
    return jax.shard_map(
        per_device,
        mesh=fine,
        in_specs=(P(blocks, None), P(blocks), P(blocks)),
        out_specs=(P(blocks), P(blocks, None)),
        check_vma=False,
    )
```

```python
import math

import jax
import jax.numpy as jnp
from jax import lax
from jax.experimental import pallas as pl
from jax.experimental.pallas import tpu as pltpu
from jax.sharding import Mesh, PartitionSpec as P

inv_temp = 10.0
epsilon = 1e-06
tile = 256
lanes = 128
quarter = 64
packed = 264
group = ("yh", "yl", "core")
sizes = {"z": 8, "x": 4, "yh": 4, "yl": 2, "core": 2}
steps = (0, 3, 1, 2)
mib = 1024 * 1024
f32, bf16 = jnp.float32, jnp.bfloat16


def halves(array):
    high = array.astype(bf16)
    low = (array - high.astype(f32)).astype(bf16)
    return high, low


def as_column(row):
    return jnp.transpose(jnp.broadcast_to(row, (lanes, row.shape[1])))


def dot(left, right, dims=((1,), (0,))):
    return lax.dot_general(left, right, (dims, ((), ())), preferred_element_type=f32)


def products(left, right, dims=((1,), (0,))):
    return dot(left[0], right[0], dims) + dot(left[0], right[1], dims) + dot(left[1], right[0], dims)


def pieces(array):
    return [array[:, at : at + lanes] for at in range(0, array.shape[1], lanes)]


def fetch(sems, *pairs):
    copies = [pltpu.make_async_copy(a, b, sems.at[i]) for i, (a, b) in enumerate(pairs)]
    for copy in copies:
        copy.start()
    return copies


def wait_all(copies):
    for copy in copies:
        copy.wait()


def blocks_of(ref):
    return [ref.at[pl.ds(at, tile), :] for at in range(0, ref.shape[0], tile)]


def info_pairs(rows, info):
    return [(rows.at[block, pl.ds(tile, 8), :], info.at[block]) for block in range(rows.shape[0])]


def member():
    return lax.axis_index("yl") * 2 + lax.axis_index("core")


def source_of(chunk):
    return lax.rem(lax.axis_index("x") + steps[chunk], 4)


def seen_ids(chunk, count):
    first = source_of(chunk) * 1024 + lax.axis_index("yh") * 256 + member() * quarter
    place = lax.broadcasted_iota(jnp.int32, (1, count), 1)
    return first + (place >> 6) * 4096 + (place & 63)


def start_kernel(
    rows, partner, cotangent, packed_rows, told, unit, norms, partner_in, cotangent_in, packed_in,
    sems,
):
    copies = fetch(
        sems,
        (rows, packed_in.at[pl.ds(0, tile), :]),
        (partner, partner_in),
        (cotangent, cotangent_in),
    )
    packed_in[tile:, :] = jnp.zeros((packed - tile, rows.shape[1]), f32)
    wait_all(copies)
    packed_in[tile : tile + 1, :] = partner_in[...].astype(f32)
    packed_in[tile + 1 : tile + 2, :] = cotangent_in[...]
    copies = fetch(sems, (packed_in, packed_rows))
    own = packed_in[pl.ds(pl.multiple_of(member() * quarter, quarter), quarter), :]
    own_norms = jnp.sqrt(jnp.sum(own * own, axis=1, keepdims=True) + epsilon)
    own_unit = own / own_norms
    unit[...] = own_unit
    norms[...] = jnp.broadcast_to(own_norms, norms.shape)
    told[...] = jnp.broadcast_to(own_unit[None], told.shape)
    wait_all(copies)


def rows_kernel(rows, high, low, partner):
    for block in range(rows.shape[0]):
        at = slice(block * tile, (block + 1) * tile)
        raw = rows[block, :tile, :]
        norms = jnp.sqrt(jnp.sum(raw * raw, axis=1, keepdims=True) + epsilon)
        high[at, :], low[at, :] = halves(raw / norms * (inv_temp * math.log2(math.e)))
        partner[at, :] = as_column(rows[block, tile : tile + 1, :]).astype(jnp.int32)


def score(chunk, at, row_high, row_low, cols, partner, count):
    scores = products((row_high[at, :], row_low[at, :]), cols, ((1,), (1,)))
    ids = seen_ids(chunk, count)
    exps = jnp.exp2(scores)
    if chunk == 0:
        first = (lax.axis_index("z") * 4 + lax.axis_index("x")) * 1024 + at.start
        row_ids = first + lax.broadcasted_iota(jnp.int32, (tile, 1), 0)
        exps = jnp.where(row_ids == ids, 0.0, exps)
    hits = [
        jnp.where(partner[at, :] == piece, part, 0.0)
        for piece, part in zip(pieces(ids), pieces(scores))
    ]
    return exps, jnp.sum(exps, axis=0, keepdims=True), sum(hits[1:], hits[0])


def send_parts(sems, at, parts, held, outs):
    rows_at = pl.ds(at.start, tile)
    for ref, part in zip(held, parts):
        ref[at, :] = part
    return fetch(sems, *[(a.at[rows_at, :], b.at[rows_at, :]) for a, b in zip(held, outs)])


def chunk_kernel(chunk, row_high, row_low, cols, partner, *refs):
    before, refs = refs[: 2 if chunk else 0], refs[2 if chunk else 0 :]
    high_out, low_out, col_sums, hits, plain, high, low, sems = refs
    count = cols.shape[0]
    parts = halves(cols[...])
    copies, totals = [], None
    for block in range(row_high.shape[0] // tile):
        at = slice(block * tile, (block + 1) * tile)
        exps, total, hit = score(chunk, at, row_high, row_low, parts, partner, count)
        totals = total if totals is None else totals + total
        exp_parts = halves(exps)
        copies += send_parts(sems.at[block], at, exp_parts, (high, low), (high_out, low_out))
        for i, (ref, value) in enumerate(zip((hits, plain), (hit, products(exp_parts, parts)))):
            ref[at, :] = value + before[i][at, :] if chunk else value
    for part, piece in enumerate(pieces(totals)):
        col_sums[part : part + 1, :] = piece
    wait_all(copies)


def last_kernel(
    row_high, row_low, cols_2, cols_3, partner, hits, plain, cotangent, sums_0, sums_1, high_2,
    low_2, high_3, low_3, told, shared, *refs,
):
    *held, sums, sems = refs
    count = cols_2.shape[0]
    outs = (high_2, low_2, high_3, low_3)
    parts = [halves(cols_2[...]), halves(cols_3[...])]
    copies, totals = [], [None, None]
    for block in range(row_high.shape[0] // tile):
        at = slice(block * tile, (block + 1) * tile)
        summed, hit = plain[at, :], hits[at, :]
        for i in range(2):
            exps, total, more = score(2 + i, at, row_high, row_low, parts[i], partner, count)
            totals[i] = total if block == 0 else totals[i] + total
            exp_parts = halves(exps)
            ends = slice(2 * i, 2 * i + 2)
            copies += send_parts(sems.at[block * 2 + i], at, exp_parts, held[ends], outs[ends])
            summed += products(exp_parts, parts[i])
            hit += more
        for part in range(tile // lanes):
            turned = jnp.transpose(hit[part * lanes : (part + 1) * lanes, :])
            row = math.log(2.0) * jnp.sum(turned, axis=0, keepdims=True)
            for side in range(2):
                k = block * 4 + part * 2 + side
                shared[k, :quarter, :] = summed[(part * 2 + side) * 64 : (part * 2 + side + 1) * 64]
                shared[k, quarter:, :] = jnp.zeros((8, shared.shape[2]), f32)
                here = row if side == 0 else pltpu.roll(row, 64, 1)
                shared[k, quarter : quarter + 1, :lanes] = here
    own = cotangent[pl.ds(lax.axis_index("yl"), 1), :]
    own = jnp.where(lax.axis_index("core") == 0, own, pltpu.roll(own, 64, 1))
    late = [jnp.concatenate(pieces(total), axis=0) for total in totals]
    for chunk, values in enumerate((sums_0[...], sums_1[...], *late)):
        for part in range(4):
            sums[pl.ds(source_of(chunk) * 4 + part, 1), :] = values[part : part + 1, :]
    sums[16:17, :] = own
    sums[17:, :] = jnp.zeros((7, lanes), f32)
    told[...] = jnp.broadcast_to(sums[...][None], told.shape)
    wait_all(copies)


def shadow_kernel(cols_0, cols_1, cols_2, cols_3, rows, out, cols_in, info, paired_rows, sems):
    cols = (cols_0, cols_1, cols_2, cols_3)
    copies = fetch(
        sems, *[(ref, cols_in.at[i]) for i, ref in enumerate(cols)], *info_pairs(rows, info)
    )
    wait_all(copies)
    partners = [as_column(info[i, 0:1, :]).astype(jnp.int32) for i in range(4)]
    for chunk in range(4):
        parts = halves(cols_in[chunk])
        ids = pieces(seen_ids(chunk, cols_in.shape[1]))
        for block, partner in enumerate(partners):
            at = slice(block * tile, (block + 1) * tile)
            ones = [(partner == piece).astype(f32).astype(bf16) for piece in ids]
            ones = jnp.concatenate(ones, axis=1)
            added = dot(ones, parts[0]) + dot(ones, parts[1])
            paired_rows[at, :] = paired_rows[at, :] + added if chunk else added
    wait_all(fetch(sems, (paired_rows, out)))


def grad_kernel(message, *refs):
    ins, (out, own_sum, *refs) = refs[:14], refs[14:]
    exps, cols, (paired_rows, rows) = ins[:8], ins[8:12], ins[12:]
    exps_in, refs = refs[:8], refs[8:]
    cols_in, paired_in, info, scales, weights, au_high, au_low, total, sems = refs
    arrivals = []
    for chunk in range(4):
        pairs = [(ref, exps_in[i]) for i, ref in enumerate(exps) if i % 4 == chunk]
        arrivals.append(fetch(sems.at[chunk], (cols[chunk], cols_in.at[chunk]), *pairs))
    last = fetch(sems.at[4], (paired_rows, paired_in), *info_pairs(rows, info))
    scales[...] = jnp.sum(message[...], axis=0)[:16, :]
    sums = []
    place = lax.broadcasted_iota(jnp.int32, (1, lanes), 1)
    for chunk in range(4):
        source = source_of(chunk)
        for z in range(0, 8, 2):
            even, odd = (message[(z + side) * 4 + source, 16:17, :] for side in range(2))
            row = chunk * 4 + z // 2
            sums.append(scales[pl.ds(source * 4 + z // 2, 1), :])
            weights[row : row + 1, :] = jnp.where(place < 64, even, pltpu.roll(odd, 64, 1))
    z = lax.axis_index("z")
    own = scales[pl.ds(lax.axis_index("x") * 4 + z // 2, 1), :]
    own_sum[...] = jnp.where(lax.rem(z, 2) == 0, own, pltpu.roll(own, 64, 1))
    columns = jnp.transpose(jnp.concatenate([weights[...] / jnp.concatenate(sums, axis=0)] * 8, axis=0))
    count = cols_in.shape[1]
    ids = []
    for chunk, arrival in enumerate(arrivals):
        arrival[0].wait()
        for part in range(4):
            scaled = cols_in[chunk, part * lanes : (part + 1) * lanes, :]
            scaled *= columns[:, chunk * 4 + part : chunk * 4 + part + 1]
            at = slice(chunk * count + part * lanes, chunk * count + (part + 1) * lanes)
            au_high[at, :], au_low[at, :] = halves(scaled)
        at = slice(chunk * count, (chunk + 1) * count)
        scaled_cols = (au_high[at, :], au_low[at, :])
        ids += pieces(seen_ids(chunk, count))
        wait_all(arrival[1:])
        for block in range(4):
            rows_at = slice(block * tile, (block + 1) * tile)
            added = products(
                (exps_in[chunk][rows_at, :], exps_in[4 + chunk][rows_at, :]), scaled_cols
            )
            total[rows_at, :] = added if chunk == 0 else total[rows_at, :] + added
    wait_all(last)
    for block in range(4):
        rows_at = slice(block * tile, (block + 1) * tile)
        partner = as_column(info[block, 0:1, :]).astype(jnp.int32)
        spread = jnp.zeros((tile, lanes), f32)
        for i, piece in enumerate(ids):
            spread += jnp.where(partner == piece, weights[i : i + 1, :], 0.0)
        weight = as_column(info[block, 1:2, :])[:, :1] + jnp.sum(spread, axis=1, keepdims=True)
        result = total[rows_at, :] - weight * paired_in[rows_at, :]
        for part in range(4):
            out[part % 2, block, part // 2] = result[part * 64 : (part + 1) * 64]


def final_kernel(parts, here, there, own_sum, cotangent, unit, norms, out):
    mine = pl.ds(pl.multiple_of(lax.axis_index("core") * (quarter + 8), 8), quarter + 8)
    shared = here[mine, :] + there[mine, :]
    own = cotangent[pl.ds(lax.axis_index("yl"), 1), :]
    own = jnp.where(lax.axis_index("core") == 0, own, pltpu.roll(own, 64, 1))
    scale = as_column(own / own_sum[...])[:quarter, :1]
    grad = inv_temp * (jnp.sum(parts[...], axis=0) + scale * shared[:quarter, :])
    along = jnp.sum(unit[...] * grad, axis=1, keepdims=True)
    out[:quarter, :] = (grad - unit[...] * along) / norms[:, :1]
    out[quarter:, :] = jnp.zeros((8, out.shape[1]), f32)
    out[quarter : quarter + 1, :lanes] = jnp.log(own_sum[...]) - shared[quarter : quarter + 1, :lanes]


vmem, anywhere = pl.BlockSpec(memory_space=pltpu.VMEM), pl.BlockSpec(memory_space=pl.ANY)


def call(kernel, outs, args, limit, cost=None, scratch=(), far=(), far_outs=()):
    args = [
        pltpu.with_memory_space_constraint(arg, pltpu.HBM) if i in far else arg
        for i, arg in enumerate(args)
    ]
    return pl.pallas_call(
        kernel,
        in_specs=[anywhere if i in far else vmem for i in range(len(args))],
        out_specs=[anywhere if i in far_outs else vmem for i in range(len(outs))],
        out_shape=[
            pltpu.HBM(*out) if i in far_outs else jax.ShapeDtypeStruct(*out)
            for i, out in enumerate(outs)
        ],
        scratch_shapes=list(scratch),
        compiler_params=pltpu.CompilerParams(vmem_limit_bytes=limit * mib),
        cost_estimate=cost,
    )(*args)


def estimate(passes, count, seen, width, exps=0):
    return pl.CostEstimate(
        flops=passes * 2 * count * seen * width,
        bytes_accessed=4 * (count * seen + (count + seen) * width),
        transcendentals=exps,
    )


def passed_along(array, by):
    return lax.ppermute(array, "x", [(i, (i + by) % 4) for i in range(4)])


def per_device(projections, partner, cotangent):
    width = projections.shape[1]
    count, seen = 4 * tile, 8 * quarter
    copies = pltpu.SemaphoreType.DMA
    info = pltpu.VMEM((4, 8, width), f32)
    packed_rows, told, own_unit, norms = call(
        start_kernel,
        [((packed, width), f32), ((8, quarter, width), f32), ((quarter, width), f32),
         ((quarter, lanes), f32)],
        (projections, partner[None], cotangent[None]),
        4,
        scratch=[pltpu.VMEM((1, tile), jnp.int32), pltpu.VMEM((1, tile), f32),
                 pltpu.VMEM((packed, width), f32), copies((3,))],
        far=(0, 1, 2),
        far_outs=(0,),
    )
    here = lax.all_to_all(told, "z", 0, 0, tiled=True).reshape(seen, width)
    rows = lax.all_gather(packed_rows, "yh")
    cols = [here, passed_along(here, 1), passed_along(here, -1), passed_along(here, 2)]
    row_high, row_low, partners = call(
        rows_kernel,
        [((count, width), bf16)] * 2 + [((count, lanes), jnp.int32)],
        (rows,),
        8,
    )
    exps_out = [((count, seen), bf16)] * 2
    row_sums = [((count, width), f32)] * 2
    own_exps = [pltpu.VMEM(*out) for out in exps_out]
    own_rows = [pltpu.VMEM(*out) for out in row_sums]
    highs, lows, col_sums, before = [], [], [], ()
    for chunk in range(2):

        def kernel(*refs, chunk=chunk):
            chunk_kernel(chunk, *refs)

        high, low, sums, *before = call(
            kernel,
            exps_out + [((seen // lanes, lanes), f32), ((count, lanes), f32)] + row_sums[:1],
            (row_high, row_low, cols[chunk], partners, *before),
            24,
            estimate(6, count, seen, width, count * seen),
            own_exps + [copies((4, 2))],
            far_outs=(0, 1),
        )
        highs.append(high)
        lows.append(low)
        col_sums.append(sums)
    hits, plain = before
    high_2, low_2, high_3, low_3, told, shared = call(
        last_kernel,
        exps_out * 2 + [((32, 24, lanes), f32), ((16, quarter + 8, width), f32)],
        (row_high, row_low, *cols[2:], partners, hits, plain, cotangent.reshape(2, lanes), *col_sums),
        32,
        estimate(6, count, 2 * seen, width, 2 * count * seen),
        own_exps * 2 + [pltpu.VMEM((24, lanes), f32), copies((8, 2))],
        far_outs=range(4),
    )
    highs += [high_2, high_3]
    lows += [low_2, low_3]
    here = lax.psum_scatter(shared.reshape(-1, width), ("yh", "yl"), tiled=True)
    there = lax.ppermute(here, "core", [(0, 1), (1, 0)])
    message = lax.all_to_all(told, ("z", "x"), 0, 0, tiled=True)
    (paired_rows,) = call(
        shadow_kernel,
        row_sums[:1],
        (*cols, rows),
        24,
        estimate(2, count, 4 * seen, width),
        [pltpu.VMEM((4, seen, width), f32), info, own_rows[0], copies((8,))],
        far=range(5),
        far_outs=(0,),
    )
    partial, own_sum = call(
        grad_kernel,
        [((2, 4, 2, quarter, width), f32), ((1, lanes), f32)],
        (message, *highs, *lows, *cols, paired_rows, rows),
        28,
        estimate(3, count, 4 * seen, width),
        own_exps * 4
        + [pltpu.VMEM((4, seen, width), f32), own_rows[0], info]
        + [pltpu.VMEM((16, lanes), f32)] * 2
        + [pltpu.VMEM((4 * seen, width), bf16)] * 2
        + [own_rows[0], copies((5, 5))],
        far=range(1, 15),
    )
    halved = jnp.sum(lax.all_to_all(partial, "core", 0, 0, tiled=True), axis=0)
    swapped = lax.all_to_all(halved.reshape(8, quarter, width), ("yh", "yl"), 0, 0, tiled=True)
    (result,) = call(
        final_kernel,
        [((quarter + 8, width), f32)],
        (swapped, here, there, own_sum, cotangent.reshape(2, lanes), own_unit, norms),
        4,
    )
    result = lax.all_gather(result, ("yl", "core"))
    return result[:, quarter, :quarter].reshape(-1), result[:, :quarter].reshape(-1, width)


def solution(mesh):
    fine = Mesh(mesh.devices.reshape(tuple(sizes.values())), tuple(sizes))
    blocks = ("z", "x", "yh")
    return jax.shard_map(
        per_device,
        mesh=fine,
        in_specs=(P(blocks, None), P(blocks), P(blocks)),
        out_specs=(P(blocks), P(blocks, None)),
        check_vma=False,
    )
```

```python
import math

import jax
import jax.numpy as jnp
from jax import lax
from jax.experimental import pallas as pl
from jax.experimental.pallas import tpu as pltpu
from jax.sharding import Mesh, PartitionSpec as P

inv_temp = 10.0
epsilon = 1e-06
tile = 256
lanes = 128
quarter = 64
packed = 264
group = ("yh", "yl", "core")
sizes = {"z": 8, "x": 4, "yh": 4, "yl": 2, "core": 2}
steps = (0, 3, 1, 2)
mib = 1024 * 1024
f32, bf16 = jnp.float32, jnp.bfloat16


def halves(array):
    high = array.astype(bf16)
    low = (array - high.astype(f32)).astype(bf16)
    return high, low


def as_column(row):
    return jnp.transpose(jnp.broadcast_to(row, (lanes, row.shape[1])))


def dot(left, right, dims=((1,), (0,))):
    return lax.dot_general(left, right, (dims, ((), ())), preferred_element_type=f32)


def products(left, right, dims=((1,), (0,))):
    return dot(left[0], right[0], dims) + dot(left[0], right[1], dims) + dot(left[1], right[0], dims)


def pieces(array):
    return [array[:, at : at + lanes] for at in range(0, array.shape[1], lanes)]


def fetch(sems, *pairs):
    copies = [pltpu.make_async_copy(a, b, sems.at[i]) for i, (a, b) in enumerate(pairs)]
    for copy in copies:
        copy.start()
    return copies


def wait_all(copies):
    for copy in copies:
        copy.wait()


def blocks_of(ref):
    return [ref.at[pl.ds(at, tile), :] for at in range(0, ref.shape[0], tile)]


def info_pairs(rows, info):
    return [(rows.at[block, pl.ds(tile, 8), :], info.at[block]) for block in range(rows.shape[0])]


def member():
    return lax.axis_index("yl") * 2 + lax.axis_index("core")


def source_of(chunk):
    return lax.rem(lax.axis_index("x") + steps[chunk], 4)


def seen_ids(chunk, count):
    first = source_of(chunk) * 1024 + lax.axis_index("yh") * 256 + member() * quarter
    place = lax.broadcasted_iota(jnp.int32, (1, count), 1)
    return first + (place >> 6) * 4096 + (place & 63)


def start_kernel(
    rows, partner, cotangent, packed_rows, told, unit, norms, partner_in, cotangent_in, packed_in,
    sems,
):
    copies = fetch(
        sems,
        (rows, packed_in.at[pl.ds(0, tile), :]),
        (partner, partner_in),
        (cotangent, cotangent_in),
    )
    packed_in[tile:, :] = jnp.zeros((packed - tile, rows.shape[1]), f32)
    wait_all(copies)
    packed_in[tile : tile + 1, :] = partner_in[...].astype(f32)
    packed_in[tile + 1 : tile + 2, :] = cotangent_in[...]
    copies = fetch(sems, (packed_in, packed_rows))
    own = packed_in[pl.ds(pl.multiple_of(member() * quarter, quarter), quarter), :]
    own_norms = jnp.sqrt(jnp.sum(own * own, axis=1, keepdims=True) + epsilon)
    own_unit = own / own_norms
    unit[...] = own_unit
    norms[...] = jnp.broadcast_to(own_norms, norms.shape)
    told[...] = jnp.broadcast_to(own_unit[None], told.shape)
    wait_all(copies)


def rows_kernel(rows, high, low, partner):
    for block in range(rows.shape[0]):
        at = slice(block * tile, (block + 1) * tile)
        raw = rows[block, :tile, :]
        norms = jnp.sqrt(jnp.sum(raw * raw, axis=1, keepdims=True) + epsilon)
        high[at, :], low[at, :] = halves(raw / norms * (inv_temp * math.log2(math.e)))
        partner[at, :] = as_column(rows[block, tile : tile + 1, :]).astype(jnp.int32)


def score(chunk, at, row_high, row_low, cols, partner, count):
    scores = products((row_high[at, :], row_low[at, :]), cols, ((1,), (1,)))
    ids = seen_ids(chunk, count)
    exps = jnp.exp2(scores)
    if chunk == 0:
        first = (lax.axis_index("z") * 4 + lax.axis_index("x")) * 1024 + at.start
        row_ids = first + lax.broadcasted_iota(jnp.int32, (tile, 1), 0)
        exps = jnp.where(row_ids == ids, 0.0, exps)
    hits = [
        jnp.where(partner[at, :] == piece, part, 0.0)
        for piece, part in zip(pieces(ids), pieces(scores))
    ]
    return exps, jnp.sum(exps, axis=0, keepdims=True), sum(hits[1:], hits[0])


def send_parts(sems, at, parts, held, outs):
    rows_at = pl.ds(at.start, tile)
    for ref, part in zip(held, parts):
        ref[at, :] = part
    return fetch(sems, *[(a.at[rows_at, :], b.at[rows_at, :]) for a, b in zip(held, outs)])


def chunk_kernel(chunk, row_high, row_low, cols, partner, *refs):
    before, refs = refs[: 2 if chunk else 0], refs[2 if chunk else 0 :]
    high_out, low_out, col_sums, hits, plain, high, low, sems = refs
    count = cols.shape[0]
    parts = halves(cols[...])
    copies, totals = [], None
    for block in range(row_high.shape[0] // tile):
        at = slice(block * tile, (block + 1) * tile)
        exps, total, hit = score(chunk, at, row_high, row_low, parts, partner, count)
        totals = total if totals is None else totals + total
        exp_parts = halves(exps)
        copies += send_parts(sems.at[block], at, exp_parts, (high, low), (high_out, low_out))
        for i, (ref, value) in enumerate(zip((hits, plain), (hit, products(exp_parts, parts)))):
            ref[at, :] = value + before[i][at, :] if chunk else value
    for part, piece in enumerate(pieces(totals)):
        col_sums[part : part + 1, :] = piece
    wait_all(copies)


def last_kernel(
    row_high, row_low, cols_2, cols_3, partner, hits, cotangent, sums_0, sums_1, high_2, low_2,
    high_3, low_3, told, hits_out, *refs,
):
    *held, sums, sems = refs
    count = cols_2.shape[0]
    outs = (high_2, low_2, high_3, low_3)
    parts = [halves(cols_2[...]), halves(cols_3[...])]
    copies, totals = [], [None, None]
    for block in range(row_high.shape[0] // tile):
        at = slice(block * tile, (block + 1) * tile)
        hit = hits[at, :]
        for i in range(2):
            exps, total, more = score(2 + i, at, row_high, row_low, parts[i], partner, count)
            totals[i] = total if block == 0 else totals[i] + total
            ends = slice(2 * i, 2 * i + 2)
            copies += send_parts(sems.at[block * 2 + i], at, halves(exps), held[ends], outs[ends])
            hit += more
        hits_out[at, :] = hit
    own = cotangent[pl.ds(lax.axis_index("yl"), 1), :]
    own = jnp.where(lax.axis_index("core") == 0, own, pltpu.roll(own, 64, 1))
    late = [jnp.concatenate(pieces(total), axis=0) for total in totals]
    for chunk, values in enumerate((sums_0[...], sums_1[...], *late)):
        for part in range(4):
            sums[pl.ds(source_of(chunk) * 4 + part, 1), :] = values[part : part + 1, :]
    sums[16:17, :] = own
    sums[17:, :] = jnp.zeros((7, lanes), f32)
    told[...] = jnp.broadcast_to(sums[...][None], told.shape)
    wait_all(copies)


def share_kernel(
    high_2, low_2, high_3, low_3, cols_2, cols_3, plain, hits, out, exps_in, cols_in, plain_in,
    hits_in, shared, sems,
):
    first = fetch(
        sems.at[4], (cols_2, cols_in.at[0]), (cols_3, cols_in.at[1]), (plain, plain_in),
        (hits, hits_in),
    )
    arrivals = []
    for block in range(4):
        at = pl.ds(block * tile, tile)
        pairs = enumerate((high_2, low_2, high_3, low_3))
        pairs = [(ref.at[at, :], exps_in.at[i, at, :]) for i, ref in pairs]
        arrivals.append(fetch(sems.at[block], *pairs))
    wait_all(first)
    parts = [halves(cols_in[i]) for i in range(2)]
    sent = []
    for block, arrival in enumerate(arrivals):
        at = slice(block * tile, (block + 1) * tile)
        wait_all(arrival)
        summed = plain_in[at, :]
        for i in range(2):
            summed += products((exps_in[2 * i, at, :], exps_in[2 * i + 1, at, :]), parts[i])
        for part in range(tile // lanes):
            turned = hits_in[at.start + part * lanes : at.start + (part + 1) * lanes, :]
            row = math.log(2.0) * jnp.sum(jnp.transpose(turned), axis=0, keepdims=True)
            for side in range(2):
                k = block * 4 + part * 2 + side
                shared[k, :quarter, :] = summed[(part * 2 + side) * 64 : (part * 2 + side + 1) * 64]
                shared[k, quarter:, :] = jnp.zeros((8, shared.shape[2]), f32)
                here = row if side == 0 else pltpu.roll(row, 64, 1)
                shared[k, quarter : quarter + 1, :lanes] = here
        ends = pl.ds(block * 4, 4)
        sent += fetch(sems.at[5 + block], (shared.at[ends], out.at[ends]))
    wait_all(sent)


def shadow_kernel(
    cols_0, cols_1, cols_2, cols_3, rows, shared, out, cols_in, info, paired_rows, sems
):
    del shared
    cols = (cols_0, cols_1, cols_2, cols_3)
    copies = fetch(
        sems, *[(ref, cols_in.at[i]) for i, ref in enumerate(cols)], *info_pairs(rows, info)
    )
    wait_all(copies)
    partners = [as_column(info[i, 0:1, :]).astype(jnp.int32) for i in range(4)]
    for chunk in range(4):
        parts = halves(cols_in[chunk])
        ids = pieces(seen_ids(chunk, cols_in.shape[1]))
        for block, partner in enumerate(partners):
            at = slice(block * tile, (block + 1) * tile)
            ones = [(partner == piece).astype(f32).astype(bf16) for piece in ids]
            ones = jnp.concatenate(ones, axis=1)
            added = dot(ones, parts[0]) + dot(ones, parts[1])
            paired_rows[at, :] = paired_rows[at, :] + added if chunk else added
    wait_all(fetch(sems, (paired_rows, out)))


def grad_kernel(message, *refs):
    ins, (out, own_sum, *refs) = refs[:14], refs[14:]
    exps, cols, (paired_rows, rows) = ins[:8], ins[8:12], ins[12:]
    exps_in, refs = refs[:8], refs[8:]
    cols_in, paired_in, info, scales, weights, au_high, au_low, total, sems = refs
    facts = fetch(sems.at[4], *info_pairs(rows, info))
    arrivals = []
    for chunk in range(4):
        pairs = [(ref, exps_in[i]) for i, ref in enumerate(exps) if i % 4 == chunk]
        arrivals.append(fetch(sems.at[chunk], (cols[chunk], cols_in.at[chunk]), *pairs))
    last = fetch(sems.at[5], (paired_rows, paired_in))
    scales[...] = jnp.sum(message[...], axis=0)[:16, :]
    sums = []
    place = lax.broadcasted_iota(jnp.int32, (1, lanes), 1)
    for chunk in range(4):
        source = source_of(chunk)
        for z in range(0, 8, 2):
            even, odd = (message[(z + side) * 4 + source, 16:17, :] for side in range(2))
            row = chunk * 4 + z // 2
            sums.append(scales[pl.ds(source * 4 + z // 2, 1), :])
            weights[row : row + 1, :] = jnp.where(place < 64, even, pltpu.roll(odd, 64, 1))
    z = lax.axis_index("z")
    own = scales[pl.ds(lax.axis_index("x") * 4 + z // 2, 1), :]
    own_sum[...] = jnp.where(lax.rem(z, 2) == 0, own, pltpu.roll(own, 64, 1))
    columns = jnp.transpose(jnp.concatenate([weights[...] / jnp.concatenate(sums, axis=0)] * 8, axis=0))
    count = cols_in.shape[1]
    ids = sum((pieces(seen_ids(chunk, count)) for chunk in range(4)), [])
    wait_all(facts)
    paired_weights = []
    for block in range(4):
        partner = as_column(info[block, 0:1, :]).astype(jnp.int32)
        spread = jnp.zeros((tile, lanes), f32)
        for i, piece in enumerate(ids):
            spread += jnp.where(partner == piece, weights[i : i + 1, :], 0.0)
        own_weight = as_column(info[block, 1:2, :])[:, :1]
        paired_weights.append(own_weight + jnp.sum(spread, axis=1, keepdims=True))
    for chunk, arrival in enumerate(arrivals):
        arrival[0].wait()
        for part in range(4):
            scaled = cols_in[chunk, part * lanes : (part + 1) * lanes, :]
            scaled *= columns[:, chunk * 4 + part : chunk * 4 + part + 1]
            at = slice(chunk * count + part * lanes, chunk * count + (part + 1) * lanes)
            au_high[at, :], au_low[at, :] = halves(scaled)
        at = slice(chunk * count, (chunk + 1) * count)
        scaled_cols = (au_high[at, :], au_low[at, :])
        wait_all(arrival[1:])
        for block in range(4):
            rows_at = slice(block * tile, (block + 1) * tile)
            added = products(
                (exps_in[chunk][rows_at, :], exps_in[4 + chunk][rows_at, :]), scaled_cols
            )
            total[rows_at, :] = added if chunk == 0 else total[rows_at, :] + added
    wait_all(last)
    for block in range(4):
        rows_at = slice(block * tile, (block + 1) * tile)
        result = total[rows_at, :] - paired_weights[block] * paired_in[rows_at, :]
        for part in range(4):
            out[part % 2, block, part // 2] = result[part * 64 : (part + 1) * 64]


def final_kernel(parts, here, there, own_sum, cotangent, unit, norms, out):
    mine = pl.ds(pl.multiple_of(lax.axis_index("core") * (quarter + 8), 8), quarter + 8)
    shared = here[mine, :] + there[mine, :]
    own = cotangent[pl.ds(lax.axis_index("yl"), 1), :]
    own = jnp.where(lax.axis_index("core") == 0, own, pltpu.roll(own, 64, 1))
    scale = as_column(own / own_sum[...])[:quarter, :1]
    grad = inv_temp * (jnp.sum(parts[...], axis=0) + scale * shared[:quarter, :])
    along = jnp.sum(unit[...] * grad, axis=1, keepdims=True)
    out[:quarter, :] = (grad - unit[...] * along) / norms[:, :1]
    out[quarter:, :] = jnp.zeros((8, out.shape[1]), f32)
    out[quarter : quarter + 1, :lanes] = jnp.log(own_sum[...]) - shared[quarter : quarter + 1, :lanes]


vmem, anywhere = pl.BlockSpec(memory_space=pltpu.VMEM), pl.BlockSpec(memory_space=pl.ANY)


def call(kernel, outs, args, limit, cost=None, scratch=(), far=(), far_outs=()):
    args = [
        pltpu.with_memory_space_constraint(arg, pltpu.HBM) if i in far else arg
        for i, arg in enumerate(args)
    ]
    return pl.pallas_call(
        kernel,
        in_specs=[anywhere if i in far else vmem for i in range(len(args))],
        out_specs=[anywhere if i in far_outs else vmem for i in range(len(outs))],
        out_shape=[
            pltpu.HBM(*out) if i in far_outs else jax.ShapeDtypeStruct(*out)
            for i, out in enumerate(outs)
        ],
        scratch_shapes=list(scratch),
        compiler_params=pltpu.CompilerParams(vmem_limit_bytes=limit * mib),
        cost_estimate=cost,
    )(*args)


def estimate(passes, count, seen, width, exps=0):
    return pl.CostEstimate(
        flops=passes * 2 * count * seen * width,
        bytes_accessed=4 * (count * seen + (count + seen) * width),
        transcendentals=exps,
    )


def passed_along(array, by):
    return lax.ppermute(array, "x", [(i, (i + by) % 4) for i in range(4)])


def per_device(projections, partner, cotangent):
    width = projections.shape[1]
    count, seen = 4 * tile, 8 * quarter
    copies = pltpu.SemaphoreType.DMA
    info = pltpu.VMEM((4, 8, width), f32)
    packed_rows, told, own_unit, norms = call(
        start_kernel,
        [((packed, width), f32), ((8, quarter, width), f32), ((quarter, width), f32),
         ((quarter, lanes), f32)],
        (projections, partner[None], cotangent[None]),
        4,
        scratch=[pltpu.VMEM((1, tile), jnp.int32), pltpu.VMEM((1, tile), f32),
                 pltpu.VMEM((packed, width), f32), copies((3,))],
        far=(0, 1, 2),
        far_outs=(0,),
    )
    here = lax.all_to_all(told, "z", 0, 0, tiled=True).reshape(seen, width)
    rows = lax.all_gather(packed_rows, "yh")
    cols = [here, passed_along(here, 1), passed_along(here, -1), passed_along(here, 2)]
    row_high, row_low, partners = call(
        rows_kernel,
        [((count, width), bf16)] * 2 + [((count, lanes), jnp.int32)],
        (rows,),
        8,
    )
    exps_out = [((count, seen), bf16)] * 2
    row_sums = [((count, width), f32)] * 2
    own_exps = [pltpu.VMEM(*out) for out in exps_out]
    own_rows = [pltpu.VMEM(*out) for out in row_sums]
    highs, lows, col_sums, before = [], [], [], ()
    for chunk in range(2):

        def kernel(*refs, chunk=chunk):
            chunk_kernel(chunk, *refs)

        high, low, sums, *before = call(
            kernel,
            exps_out + [((seen // lanes, lanes), f32), ((count, lanes), f32)] + row_sums[:1],
            (row_high, row_low, cols[chunk], partners, *before),
            24,
            estimate(6, count, seen, width, count * seen),
            own_exps + [copies((4, 2))],
            far_outs=(0, 1),
        )
        highs.append(high)
        lows.append(low)
        col_sums.append(sums)
    hits, plain = before
    high_2, low_2, high_3, low_3, told, hits = call(
        last_kernel,
        exps_out * 2 + [((32, 24, lanes), f32), ((count, lanes), f32)],
        (row_high, row_low, *cols[2:], partners, hits, cotangent.reshape(2, lanes), *col_sums),
        32,
        estimate(3, count, 2 * seen, width, 2 * count * seen),
        own_exps * 2 + [pltpu.VMEM((24, lanes), f32), copies((8, 2))],
        far_outs=range(4),
    )
    highs += [high_2, high_3]
    lows += [low_2, low_3]
    (shared,) = call(
        share_kernel,
        [((16, quarter + 8, width), f32)],
        (high_2, low_2, high_3, low_3, *cols[2:], plain, hits),
        24,
        estimate(3, count, 2 * seen, width),
        [pltpu.VMEM((4, count, seen), bf16), pltpu.VMEM((2, seen, width), f32), own_rows[0],
         pltpu.VMEM((count, lanes), f32), pltpu.VMEM((16, quarter + 8, width), f32),
         copies((9, 4))],
        far=range(8),
        far_outs=(0,),
    )
    here = lax.psum_scatter(shared.reshape(-1, width), ("yh", "yl"), tiled=True)
    there = lax.ppermute(here, "core", [(0, 1), (1, 0)])
    message = lax.all_to_all(told, ("z", "x"), 0, 0, tiled=True)
    (paired_rows,) = call(
        shadow_kernel,
        row_sums[:1],
        (*cols, rows, shared),
        24,
        estimate(2, count, 4 * seen, width),
        [pltpu.VMEM((4, seen, width), f32), info, own_rows[0], copies((8,))],
        far=range(6),
        far_outs=(0,),
    )
    partial, own_sum = call(
        grad_kernel,
        [((2, 4, 2, quarter, width), f32), ((1, lanes), f32)],
        (message, *highs, *lows, *cols, paired_rows, rows),
        28,
        estimate(30, count, 4 * seen, width),
        own_exps * 4
        + [pltpu.VMEM((4, seen, width), f32), own_rows[0], info]
        + [pltpu.VMEM((16, lanes), f32)] * 2
        + [pltpu.VMEM((4 * seen, width), bf16)] * 2
        + [own_rows[0], copies((6, 4))],
        far=range(1, 15),
    )
    halved = jnp.sum(lax.all_to_all(partial, "core", 0, 0, tiled=True), axis=0)
    swapped = lax.all_to_all(halved.reshape(8, quarter, width), ("yh", "yl"), 0, 0, tiled=True)
    (result,) = call(
        final_kernel,
        [((quarter + 8, width), f32)],
        (swapped, here, there, own_sum, cotangent.reshape(2, lanes), own_unit, norms),
        4,
    )
    result = lax.all_gather(result, ("yl", "core"))
    return result[:, quarter, :quarter].reshape(-1), result[:, :quarter].reshape(-1, width)


def solution(mesh):
    fine = Mesh(mesh.devices.reshape(tuple(sizes.values())), tuple(sizes))
    blocks = ("z", "x", "yh")
    return jax.shard_map(
        per_device,
        mesh=fine,
        in_specs=(P(blocks, None), P(blocks), P(blocks)),
        out_specs=(P(blocks), P(blocks, None)),
        check_vma=False,
    )
```

```python
import math

import jax
import jax.numpy as jnp
from jax import lax
from jax.experimental import pallas as pl
from jax.experimental.pallas import tpu as pltpu
from jax.sharding import Mesh, PartitionSpec as P

inv_temp = 10.0
epsilon = 1e-06
tile = 256
lanes = 128
quarter = 64
packed = 264
group = ("yh", "yl", "core")
sizes = {"z": 8, "x": 4, "yh": 4, "yl": 2, "core": 2}
steps = (0, 3, 1, 2)
mib = 1024 * 1024
f32, bf16 = jnp.float32, jnp.bfloat16


def halves(array):
    high = array.astype(bf16)
    low = (array - high.astype(f32)).astype(bf16)
    return high, low


def as_column(row):
    return jnp.transpose(jnp.broadcast_to(row, (lanes, row.shape[1])))


def dot(left, right, dims=((1,), (0,))):
    return lax.dot_general(left, right, (dims, ((), ())), preferred_element_type=f32)


def products(left, right, dims=((1,), (0,))):
    return dot(left[0], right[0], dims) + dot(left[0], right[1], dims) + dot(left[1], right[0], dims)


def pieces(array):
    return [array[:, at : at + lanes] for at in range(0, array.shape[1], lanes)]


def fetch(sems, *pairs):
    copies = [pltpu.make_async_copy(a, b, sems.at[i]) for i, (a, b) in enumerate(pairs)]
    for copy in copies:
        copy.start()
    return copies


def wait_all(copies):
    for copy in copies:
        copy.wait()


def blocks_of(ref):
    return [ref.at[pl.ds(at, tile), :] for at in range(0, ref.shape[0], tile)]


def info_pairs(rows, info):
    return [(rows.at[block, pl.ds(tile, 8), :], info.at[block]) for block in range(rows.shape[0])]


def member():
    return lax.axis_index("yl") * 2 + lax.axis_index("core")


def source_of(chunk):
    return lax.rem(lax.axis_index("x") + steps[chunk], 4)


def seen_ids(chunk, count):
    first = source_of(chunk) * 1024 + lax.axis_index("yh") * 256 + member() * quarter
    place = lax.broadcasted_iota(jnp.int32, (1, count), 1)
    return first + (place >> 6) * 4096 + (place & 63)


def start_kernel(
    rows, partner, cotangent, packed_rows, told, unit, norms, partner_in, cotangent_in, packed_in,
    sems,
):
    copies = fetch(
        sems,
        (rows, packed_in.at[pl.ds(0, tile), :]),
        (partner, partner_in),
        (cotangent, cotangent_in),
    )
    packed_in[tile:, :] = jnp.zeros((packed - tile, rows.shape[1]), f32)
    wait_all(copies)
    packed_in[tile : tile + 1, :] = partner_in[...].astype(f32)
    packed_in[tile + 1 : tile + 2, :] = cotangent_in[...]
    copies = fetch(sems, (packed_in, packed_rows))
    own = packed_in[pl.ds(pl.multiple_of(member() * quarter, quarter), quarter), :]
    own_norms = jnp.sqrt(jnp.sum(own * own, axis=1, keepdims=True) + epsilon)
    own_unit = own / own_norms
    unit[...] = own_unit
    norms[...] = jnp.broadcast_to(own_norms, norms.shape)
    told[...] = jnp.broadcast_to(own_unit[None], told.shape)
    wait_all(copies)


def rows_kernel(rows, high, low, partner):
    for block in range(rows.shape[0]):
        at = slice(block * tile, (block + 1) * tile)
        raw = rows[block, :tile, :]
        norms = jnp.sqrt(jnp.sum(raw * raw, axis=1, keepdims=True) + epsilon)
        high[at, :], low[at, :] = halves(raw / norms * (inv_temp * math.log2(math.e)))
        partner[at, :] = as_column(rows[block, tile : tile + 1, :]).astype(jnp.int32)


def score(chunk, at, row_high, row_low, cols, partner, count):
    scores = products((row_high[at, :], row_low[at, :]), cols, ((1,), (1,)))
    ids = seen_ids(chunk, count)
    exps = jnp.exp2(scores)
    if chunk == 0:
        first = (lax.axis_index("z") * 4 + lax.axis_index("x")) * 1024 + at.start
        row_ids = first + lax.broadcasted_iota(jnp.int32, (tile, 1), 0)
        exps = jnp.where(row_ids == ids, 0.0, exps)
    hits = [
        jnp.where(partner[at, :] == piece, part, 0.0)
        for piece, part in zip(pieces(ids), pieces(scores))
    ]
    return exps, jnp.sum(exps, axis=0, keepdims=True), sum(hits[1:], hits[0])


def send_parts(sems, at, parts, held, outs):
    rows_at = pl.ds(at.start, tile)
    for ref, part in zip(held, parts):
        ref[at, :] = part
    return fetch(sems, *[(a.at[rows_at, :], b.at[rows_at, :]) for a, b in zip(held, outs)])


def chunk_kernel(chunk, row_high, row_low, cols, partner, *refs):
    before, refs = refs[: 2 if chunk else 0], refs[2 if chunk else 0 :]
    high_out, low_out, col_sums, hits, plain, high, low, sems = refs
    count = cols.shape[0]
    parts = halves(cols[...])
    copies, totals = [], None
    for block in range(row_high.shape[0] // tile):
        at = slice(block * tile, (block + 1) * tile)
        exps, total, hit = score(chunk, at, row_high, row_low, parts, partner, count)
        totals = total if totals is None else totals + total
        exp_parts = halves(exps)
        copies += send_parts(sems.at[block], at, exp_parts, (high, low), (high_out, low_out))
        for i, (ref, value) in enumerate(zip((hits, plain), (hit, products(exp_parts, parts)))):
            ref[at, :] = value + before[i][at, :] if chunk else value
    for part, piece in enumerate(pieces(totals)):
        col_sums[part : part + 1, :] = piece
    wait_all(copies)


def last_kernel(
    row_high, row_low, cols_2, cols_3, partner, hits, plain, cotangent, sums_0, sums_1, high_2,
    low_2, high_3, low_3, told, shared_out, *refs,
):
    *held, sums, shared, sems, shared_sems = refs
    count = cols_2.shape[0]
    outs = (high_2, low_2, high_3, low_3)
    parts = [halves(cols_2[...]), halves(cols_3[...])]
    copies, totals = [], [None, None]
    for block in range(row_high.shape[0] // tile):
        at = slice(block * tile, (block + 1) * tile)
        summed, hit = plain[at, :], hits[at, :]
        for i in range(2):
            exps, total, more = score(2 + i, at, row_high, row_low, parts[i], partner, count)
            totals[i] = total if block == 0 else totals[i] + total
            exp_parts = halves(exps)
            ends = slice(2 * i, 2 * i + 2)
            copies += send_parts(sems.at[block * 2 + i], at, exp_parts, held[ends], outs[ends])
            summed += products(exp_parts, parts[i])
            hit += more
        for part in range(tile // lanes):
            turned = jnp.transpose(hit[part * lanes : (part + 1) * lanes, :])
            row = math.log(2.0) * jnp.sum(turned, axis=0, keepdims=True)
            for side in range(2):
                k = block * 4 + part * 2 + side
                shared[k, :quarter, :] = summed[(part * 2 + side) * 64 : (part * 2 + side + 1) * 64]
                shared[k, quarter:, :] = jnp.zeros((8, shared.shape[2]), f32)
                here = row if side == 0 else pltpu.roll(row, 64, 1)
                shared[k, quarter : quarter + 1, :lanes] = here
        ends = pl.ds(block * 4, 4)
        copies += fetch(shared_sems.at[block], (shared.at[ends], shared_out.at[ends]))
    own = cotangent[pl.ds(lax.axis_index("yl"), 1), :]
    own = jnp.where(lax.axis_index("core") == 0, own, pltpu.roll(own, 64, 1))
    late = [jnp.concatenate(pieces(total), axis=0) for total in totals]
    for chunk, values in enumerate((sums_0[...], sums_1[...], *late)):
        for part in range(4):
            sums[pl.ds(source_of(chunk) * 4 + part, 1), :] = values[part : part + 1, :]
    sums[16:17, :] = own
    sums[17:, :] = jnp.zeros((7, lanes), f32)
    told[...] = jnp.broadcast_to(sums[...][None], told.shape)
    wait_all(copies)


def shadow_kernel(cols_0, cols_1, cols_2, cols_3, rows, out, cols_in, info, paired_rows, sems):
    cols = (cols_0, cols_1, cols_2, cols_3)
    copies = fetch(
        sems, *[(ref, cols_in.at[i]) for i, ref in enumerate(cols)], *info_pairs(rows, info)
    )
    wait_all(copies)
    partners = [as_column(info[i, 0:1, :]).astype(jnp.int32) for i in range(4)]
    for chunk in range(4):
        parts = halves(cols_in[chunk])
        ids = pieces(seen_ids(chunk, cols_in.shape[1]))
        for block, partner in enumerate(partners):
            at = slice(block * tile, (block + 1) * tile)
            ones = [(partner == piece).astype(f32).astype(bf16) for piece in ids]
            ones = jnp.concatenate(ones, axis=1)
            added = dot(ones, parts[0]) + dot(ones, parts[1])
            paired_rows[at, :] = paired_rows[at, :] + added if chunk else added
    wait_all(fetch(sems, (paired_rows, out)))


def grad_kernel(message, *refs):
    ins, (out, own_sum, *refs) = refs[:14], refs[14:]
    exps, cols, (paired_rows, rows) = ins[:8], ins[8:12], ins[12:]
    exps_in, refs = refs[:8], refs[8:]
    cols_in, paired_in, info, scales, weights, au_high, au_low, total, sems = refs
    facts = fetch(sems.at[4], *info_pairs(rows, info))
    arrivals = []
    for chunk in range(4):
        pairs = [(ref, exps_in[i]) for i, ref in enumerate(exps) if i % 4 == chunk]
        arrivals.append(fetch(sems.at[chunk], (cols[chunk], cols_in.at[chunk]), *pairs))
    last = fetch(sems.at[5], (paired_rows, paired_in))
    scales[...] = jnp.sum(message[...], axis=0)[:16, :]
    sums = []
    place = lax.broadcasted_iota(jnp.int32, (1, lanes), 1)
    for chunk in range(4):
        source = source_of(chunk)
        for z in range(0, 8, 2):
            even, odd = (message[(z + side) * 4 + source, 16:17, :] for side in range(2))
            row = chunk * 4 + z // 2
            sums.append(scales[pl.ds(source * 4 + z // 2, 1), :])
            weights[row : row + 1, :] = jnp.where(place < 64, even, pltpu.roll(odd, 64, 1))
    z = lax.axis_index("z")
    own = scales[pl.ds(lax.axis_index("x") * 4 + z // 2, 1), :]
    own_sum[...] = jnp.where(lax.rem(z, 2) == 0, own, pltpu.roll(own, 64, 1))
    columns = jnp.transpose(jnp.concatenate([weights[...] / jnp.concatenate(sums, axis=0)] * 8, axis=0))
    count = cols_in.shape[1]
    ids = sum((pieces(seen_ids(chunk, count)) for chunk in range(4)), [])
    wait_all(facts)
    paired_weights = []
    for block in range(4):
        partner = as_column(info[block, 0:1, :]).astype(jnp.int32)
        spread = jnp.zeros((tile, lanes), f32)
        for i, piece in enumerate(ids):
            spread += jnp.where(partner == piece, weights[i : i + 1, :], 0.0)
        own_weight = as_column(info[block, 1:2, :])[:, :1]
        paired_weights.append(own_weight + jnp.sum(spread, axis=1, keepdims=True))
    for chunk, arrival in enumerate(arrivals):
        arrival[0].wait()
        for part in range(4):
            scaled = cols_in[chunk, part * lanes : (part + 1) * lanes, :]
            scaled *= columns[:, chunk * 4 + part : chunk * 4 + part + 1]
            at = slice(chunk * count + part * lanes, chunk * count + (part + 1) * lanes)
            au_high[at, :], au_low[at, :] = halves(scaled)
        at = slice(chunk * count, (chunk + 1) * count)
        scaled_cols = (au_high[at, :], au_low[at, :])
        wait_all(arrival[1:])
        for block in range(4):
            rows_at = slice(block * tile, (block + 1) * tile)
            added = products(
                (exps_in[chunk][rows_at, :], exps_in[4 + chunk][rows_at, :]), scaled_cols
            )
            total[rows_at, :] = added if chunk == 0 else total[rows_at, :] + added
    wait_all(last)
    for block in range(4):
        rows_at = slice(block * tile, (block + 1) * tile)
        result = total[rows_at, :] - paired_weights[block] * paired_in[rows_at, :]
        for part in range(4):
            out[part % 2, block, part // 2] = result[part * 64 : (part + 1) * 64]


def losses_kernel(here, there, own_sum, cotangent, scaled, losses):
    mine = pl.ds(pl.multiple_of(lax.axis_index("core") * (quarter + 8), 8), quarter + 8)
    shared = here[mine, :] + there[mine, :]
    own = cotangent[pl.ds(lax.axis_index("yl"), 1), :]
    own = jnp.where(lax.axis_index("core") == 0, own, pltpu.roll(own, 64, 1))
    scaled[...] = as_column(own / own_sum[...])[:quarter, :1] * shared[:quarter, :]
    row = jnp.log(own_sum[...]) - shared[quarter : quarter + 1, :lanes]
    losses[...] = jnp.broadcast_to(row, losses.shape)


def final_kernel(parts, scaled, unit, norms, losses, out):
    del losses
    grad = inv_temp * (jnp.sum(parts[...], axis=0) + scaled[...])
    along = jnp.sum(unit[...] * grad, axis=1, keepdims=True)
    out[...] = (grad - unit[...] * along) / norms[:, :1]


vmem, anywhere = pl.BlockSpec(memory_space=pltpu.VMEM), pl.BlockSpec(memory_space=pl.ANY)


def call(kernel, outs, args, limit, cost=None, scratch=(), far=(), far_outs=()):
    args = [
        pltpu.with_memory_space_constraint(arg, pltpu.HBM) if i in far else arg
        for i, arg in enumerate(args)
    ]
    return pl.pallas_call(
        kernel,
        in_specs=[anywhere if i in far else vmem for i in range(len(args))],
        out_specs=[anywhere if i in far_outs else vmem for i in range(len(outs))],
        out_shape=[
            pltpu.HBM(*out) if i in far_outs else jax.ShapeDtypeStruct(*out)
            for i, out in enumerate(outs)
        ],
        scratch_shapes=list(scratch),
        compiler_params=pltpu.CompilerParams(vmem_limit_bytes=limit * mib),
        cost_estimate=cost,
    )(*args)


def estimate(passes, count, seen, width, exps=0):
    return pl.CostEstimate(
        flops=passes * 2 * count * seen * width,
        bytes_accessed=4 * (count * seen + (count + seen) * width),
        transcendentals=exps,
    )


def passed_along(array, by):
    return lax.ppermute(array, "x", [(i, (i + by) % 4) for i in range(4)])


def per_device(projections, partner, cotangent):
    width = projections.shape[1]
    count, seen = 4 * tile, 8 * quarter
    copies = pltpu.SemaphoreType.DMA
    info = pltpu.VMEM((4, 8, width), f32)
    packed_rows, told, own_unit, norms = call(
        start_kernel,
        [((packed, width), f32), ((8, quarter, width), f32), ((quarter, width), f32),
         ((quarter, lanes), f32)],
        (projections, partner[None], cotangent[None]),
        4,
        scratch=[pltpu.VMEM((1, tile), jnp.int32), pltpu.VMEM((1, tile), f32),
                 pltpu.VMEM((packed, width), f32), copies((3,))],
        far=(0, 1, 2),
        far_outs=(0,),
    )
    here = lax.all_to_all(told, "z", 0, 0, tiled=True).reshape(seen, width)
    rows = lax.all_gather(packed_rows, "yh")
    cols = [here, passed_along(here, 1), passed_along(here, -1), passed_along(here, 2)]
    row_high, row_low, partners = call(
        rows_kernel,
        [((count, width), bf16)] * 2 + [((count, lanes), jnp.int32)],
        (rows,),
        8,
    )
    exps_out = [((count, seen), bf16)] * 2
    row_sums = [((count, width), f32)] * 2
    own_exps = [pltpu.VMEM(*out) for out in exps_out]
    own_rows = [pltpu.VMEM(*out) for out in row_sums]
    highs, lows, col_sums, before = [], [], [], ()
    for chunk in range(2):

        def kernel(*refs, chunk=chunk):
            chunk_kernel(chunk, *refs)

        high, low, sums, *before = call(
            kernel,
            exps_out + [((seen // lanes, lanes), f32), ((count, lanes), f32)] + row_sums[:1],
            (row_high, row_low, cols[chunk], partners, *before),
            24,
            estimate(6, count, seen, width, count * seen),
            own_exps + [copies((4, 2))],
            far_outs=(0, 1),
        )
        highs.append(high)
        lows.append(low)
        col_sums.append(sums)
    hits, plain = before
    high_2, low_2, high_3, low_3, told, shared = call(
        last_kernel,
        exps_out * 2 + [((32, 24, lanes), f32), ((16, quarter + 8, width), f32)],
        (row_high, row_low, *cols[2:], partners, hits, plain, cotangent.reshape(2, lanes), *col_sums),
        32,
        estimate(6, count, 2 * seen, width, 2 * count * seen),
        own_exps * 2
        + [pltpu.VMEM((24, lanes), f32), pltpu.VMEM((16, quarter + 8, width), f32)]
        + [copies((8, 2)), copies((4, 1))],
        far_outs=(0, 1, 2, 3, 5),
    )
    highs += [high_2, high_3]
    lows += [low_2, low_3]
    here = lax.psum_scatter(shared.reshape(-1, width), ("yh", "yl"), tiled=True)
    there = lax.ppermute(here, "core", [(0, 1), (1, 0)])
    message = lax.all_to_all(told, ("z", "x"), 0, 0, tiled=True)
    (paired_rows,) = call(
        shadow_kernel,
        row_sums[:1],
        (*cols, rows),
        24,
        estimate(2, count, 4 * seen, width),
        [pltpu.VMEM((4, seen, width), f32), info, own_rows[0], copies((8,))],
        far=range(5),
        far_outs=(0,),
    )
    partial, own_sum = call(
        grad_kernel,
        [((2, 4, 2, quarter, width), f32), ((1, lanes), f32)],
        (message, *highs, *lows, *cols, paired_rows, rows),
        28,
        estimate(3, count, 4 * seen, width),
        own_exps * 4
        + [pltpu.VMEM((4, seen, width), f32), own_rows[0], info]
        + [pltpu.VMEM((16, lanes), f32)] * 2
        + [pltpu.VMEM((4 * seen, width), bf16)] * 2
        + [own_rows[0], copies((6, 4))],
        far=range(1, 15),
    )
    halved = jnp.sum(lax.all_to_all(partial, "core", 0, 0, tiled=True), axis=0)
    swapped = lax.all_to_all(halved.reshape(8, quarter, width), ("yh", "yl"), 0, 0, tiled=True)
    scaled, losses = call(
        losses_kernel,
        [((quarter, width), f32), ((8, lanes), f32)],
        (here, there, own_sum, cotangent.reshape(2, lanes)),
        4,
    )
    losses = lax.all_gather(losses, ("yl", "core"))[:, 0, :quarter].reshape(-1)
    (grads,) = call(
        final_kernel,
        [((quarter, width), f32)],
        (swapped, scaled, own_unit, norms, losses[None]),
        4,
        far=(4,),
    )
    return losses, lax.all_gather(grads, ("yl", "core"), tiled=True)


def solution(mesh):
    fine = Mesh(mesh.devices.reshape(tuple(sizes.values())), tuple(sizes))
    blocks = ("z", "x", "yh")
    return jax.shard_map(
        per_device,
        mesh=fine,
        in_specs=(P(blocks, None), P(blocks), P(blocks)),
        out_specs=(P(blocks), P(blocks, None)),
        check_vma=False,
    )
```

```python
import math

import jax
import jax.numpy as jnp
from jax import lax
from jax.experimental import pallas as pl
from jax.experimental.pallas import tpu as pltpu
from jax.sharding import Mesh, PartitionSpec as P

inv_temp = 10.0
epsilon = 1e-06
tile = 256
lanes = 128
quarter = 64
packed = 264
group = ("yh", "yl", "core")
sizes = {"z": 8, "x": 4, "yh": 4, "yl": 2, "core": 2}
steps = (0, 3, 1, 2)
mib = 1024 * 1024
f32, bf16 = jnp.float32, jnp.bfloat16


def halves(array):
    high = array.astype(bf16)
    low = (array - high.astype(f32)).astype(bf16)
    return high, low


def as_column(row):
    return jnp.transpose(jnp.broadcast_to(row, (lanes, row.shape[1])))


def dot(left, right, dims=((1,), (0,))):
    return lax.dot_general(left, right, (dims, ((), ())), preferred_element_type=f32)


def products(left, right, dims=((1,), (0,))):
    return dot(left[0], right[0], dims) + dot(left[0], right[1], dims) + dot(left[1], right[0], dims)


def pieces(array):
    return [array[:, at : at + lanes] for at in range(0, array.shape[1], lanes)]


def fetch(sems, *pairs):
    copies = [pltpu.make_async_copy(a, b, sems.at[i]) for i, (a, b) in enumerate(pairs)]
    for copy in copies:
        copy.start()
    return copies


def wait_all(copies):
    for copy in copies:
        copy.wait()


def blocks_of(ref):
    return [ref.at[pl.ds(at, tile), :] for at in range(0, ref.shape[0], tile)]


def info_pairs(rows, info):
    return [(rows.at[block, pl.ds(tile, 8), :], info.at[block]) for block in range(rows.shape[0])]


def member():
    return lax.axis_index("yl") * 2 + lax.axis_index("core")


def source_of(chunk):
    return lax.rem(lax.axis_index("x") + steps[chunk], 4)


def seen_ids(chunk, count):
    first = source_of(chunk) * 1024 + lax.axis_index("yh") * 256 + member() * quarter
    place = lax.broadcasted_iota(jnp.int32, (1, count), 1)
    return first + (place >> 6) * 4096 + (place & 63)


def start_kernel(
    rows, partner, cotangent, packed_rows, told, unit, norms, partner_in, cotangent_in, packed_in,
    sems,
):
    copies = fetch(
        sems,
        (rows, packed_in.at[pl.ds(0, tile), :]),
        (partner, partner_in),
        (cotangent, cotangent_in),
    )
    packed_in[tile:, :] = jnp.zeros((packed - tile, rows.shape[1]), f32)
    wait_all(copies)
    packed_in[tile : tile + 1, :] = partner_in[...].astype(f32)
    packed_in[tile + 1 : tile + 2, :] = cotangent_in[...]
    copies = fetch(sems, (packed_in, packed_rows))
    own = packed_in[pl.ds(pl.multiple_of(member() * quarter, quarter), quarter), :]
    own_norms = jnp.sqrt(jnp.sum(own * own, axis=1, keepdims=True) + epsilon)
    own_unit = own / own_norms
    unit[...] = own_unit
    norms[...] = jnp.broadcast_to(own_norms, norms.shape)
    told[...] = jnp.broadcast_to(own_unit[None], told.shape)
    wait_all(copies)


def rows_kernel(rows, high, low, partner):
    for block in range(rows.shape[0]):
        at = slice(block * tile, (block + 1) * tile)
        raw = rows[block, :tile, :]
        norms = jnp.sqrt(jnp.sum(raw * raw, axis=1, keepdims=True) + epsilon)
        high[at, :], low[at, :] = halves(raw / norms * (inv_temp * math.log2(math.e)))
        partner[at, :] = as_column(rows[block, tile : tile + 1, :]).astype(jnp.int32)


def score(chunk, at, row_high, row_low, cols, partner, count):
    scores = products((row_high[at, :], row_low[at, :]), cols, ((1,), (1,)))
    ids = seen_ids(chunk, count)
    exps = jnp.exp2(scores)
    if chunk == 0:
        first = (lax.axis_index("z") * 4 + lax.axis_index("x")) * 1024 + at.start
        row_ids = first + lax.broadcasted_iota(jnp.int32, (tile, 1), 0)
        exps = jnp.where(row_ids == ids, 0.0, exps)
    hits = [
        jnp.where(partner[at, :] == piece, part, 0.0)
        for piece, part in zip(pieces(ids), pieces(scores))
    ]
    return exps, jnp.sum(exps, axis=0, keepdims=True), sum(hits[1:], hits[0])


def send_parts(sems, at, parts, held, outs):
    rows_at = pl.ds(at.start, tile)
    for ref, part in zip(held, parts):
        ref[at, :] = part
    return fetch(sems, *[(a.at[rows_at, :], b.at[rows_at, :]) for a, b in zip(held, outs)])


def chunk_kernel(chunk, row_high, row_low, cols, partner, *refs):
    before, refs = refs[: 2 if chunk else 0], refs[2 if chunk else 0 :]
    high_out, low_out, col_sums, hits, plain, high, low, sems = refs
    count = cols.shape[0]
    parts = halves(cols[...])
    copies, totals = [], None
    for block in range(row_high.shape[0] // tile):
        at = slice(block * tile, (block + 1) * tile)
        exps, total, hit = score(chunk, at, row_high, row_low, parts, partner, count)
        totals = total if totals is None else totals + total
        exp_parts = halves(exps)
        copies += send_parts(sems.at[block], at, exp_parts, (high, low), (high_out, low_out))
        for i, (ref, value) in enumerate(zip((hits, plain), (hit, products(exp_parts, parts)))):
            ref[at, :] = value + before[i][at, :] if chunk else value
    for part, piece in enumerate(pieces(totals)):
        col_sums[part : part + 1, :] = piece
    wait_all(copies)


def last_kernel(
    row_high, row_low, cols_2, cols_3, partner, hits, plain, cotangent, sums_0, sums_1, high_2,
    low_2, high_3, low_3, told_out, shared_out, *refs,
):
    *held, sums, told, shared, sems, late_sems = refs
    count = cols_2.shape[0]
    outs = (high_2, low_2, high_3, low_3)
    parts = [halves(cols_2[...]), halves(cols_3[...])]
    blocks = [slice(at, at + tile) for at in range(0, row_high.shape[0], tile)]
    copies, totals, all_hits = [], [None, None], []
    for block, at in enumerate(blocks):
        hit = hits[at, :]
        for i in range(2):
            exps, total, more = score(2 + i, at, row_high, row_low, parts[i], partner, count)
            totals[i] = total if block == 0 else totals[i] + total
            ends = slice(2 * i, 2 * i + 2)
            copies += send_parts(sems.at[block * 2 + i], at, halves(exps), held[ends], outs[ends])
            hit += more
        all_hits.append(hit)
    own = cotangent[pl.ds(lax.axis_index("yl"), 1), :]
    own = jnp.where(lax.axis_index("core") == 0, own, pltpu.roll(own, 64, 1))
    late = [jnp.concatenate(pieces(total), axis=0) for total in totals]
    for chunk, values in enumerate((sums_0[...], sums_1[...], *late)):
        for part in range(4):
            sums[pl.ds(source_of(chunk) * 4 + part, 1), :] = values[part : part + 1, :]
    sums[16:17, :] = own
    sums[17:, :] = jnp.zeros((7, lanes), f32)
    told[...] = jnp.broadcast_to(sums[...][None], told.shape)
    copies += fetch(late_sems.at[4], (told, told_out))
    for block, at in enumerate(blocks):
        summed = plain[at, :]
        for i in range(2):
            summed += products((held[2 * i][at, :], held[2 * i + 1][at, :]), parts[i])
        for part in range(tile // lanes):
            turned = jnp.transpose(all_hits[block][part * lanes : (part + 1) * lanes, :])
            row = math.log(2.0) * jnp.sum(turned, axis=0, keepdims=True)
            for side in range(2):
                k = block * 4 + part * 2 + side
                shared[k, :quarter, :] = summed[(part * 2 + side) * 64 : (part * 2 + side + 1) * 64]
                shared[k, quarter:, :] = jnp.zeros((8, shared.shape[2]), f32)
                here = row if side == 0 else pltpu.roll(row, 64, 1)
                shared[k, quarter : quarter + 1, :lanes] = here
        ends = pl.ds(block * 4, 4)
        copies += fetch(late_sems.at[block], (shared.at[ends], shared_out.at[ends]))
    wait_all(copies)


def shadow_kernel(cols_0, cols_1, cols_2, cols_3, rows, out, cols_in, info, paired_rows, sems):
    cols = (cols_0, cols_1, cols_2, cols_3)
    copies = fetch(
        sems, *[(ref, cols_in.at[i]) for i, ref in enumerate(cols)], *info_pairs(rows, info)
    )
    wait_all(copies)
    partners = [as_column(info[i, 0:1, :]).astype(jnp.int32) for i in range(4)]
    for chunk in range(4):
        parts = halves(cols_in[chunk])
        ids = pieces(seen_ids(chunk, cols_in.shape[1]))
        for block, partner in enumerate(partners):
            at = slice(block * tile, (block + 1) * tile)
            ones = [(partner == piece).astype(f32).astype(bf16) for piece in ids]
            ones = jnp.concatenate(ones, axis=1)
            added = dot(ones, parts[0]) + dot(ones, parts[1])
            paired_rows[at, :] = paired_rows[at, :] + added if chunk else added
    wait_all(fetch(sems, (paired_rows, out)))


def grad_kernel(message, *refs):
    ins, (out, own_sum, *refs) = refs[:14], refs[14:]
    exps, cols, (paired_rows, rows) = ins[:8], ins[8:12], ins[12:]
    exps_in, refs = refs[:8], refs[8:]
    cols_in, paired_in, info, scales, weights, au_high, au_low, total, sems = refs
    facts = fetch(sems.at[4], *info_pairs(rows, info))
    arrivals = []
    for chunk in range(4):
        pairs = [(ref, exps_in[i]) for i, ref in enumerate(exps) if i % 4 == chunk]
        arrivals.append(fetch(sems.at[chunk], (cols[chunk], cols_in.at[chunk]), *pairs))
    last = fetch(sems.at[5], (paired_rows, paired_in))
    scales[...] = jnp.sum(message[...], axis=0)[:16, :]
    sums = []
    place = lax.broadcasted_iota(jnp.int32, (1, lanes), 1)
    for chunk in range(4):
        source = source_of(chunk)
        for z in range(0, 8, 2):
            even, odd = (message[(z + side) * 4 + source, 16:17, :] for side in range(2))
            row = chunk * 4 + z // 2
            sums.append(scales[pl.ds(source * 4 + z // 2, 1), :])
            weights[row : row + 1, :] = jnp.where(place < 64, even, pltpu.roll(odd, 64, 1))
    z = lax.axis_index("z")
    own = scales[pl.ds(lax.axis_index("x") * 4 + z // 2, 1), :]
    own_sum[...] = jnp.where(lax.rem(z, 2) == 0, own, pltpu.roll(own, 64, 1))
    columns = jnp.transpose(jnp.concatenate([weights[...] / jnp.concatenate(sums, axis=0)] * 8, axis=0))
    count = cols_in.shape[1]
    ids = sum((pieces(seen_ids(chunk, count)) for chunk in range(4)), [])
    wait_all(facts)
    paired_weights = []
    for block in range(4):
        partner = as_column(info[block, 0:1, :]).astype(jnp.int32)
        spread = jnp.zeros((tile, lanes), f32)
        for i, piece in enumerate(ids):
            spread += jnp.where(partner == piece, weights[i : i + 1, :], 0.0)
        own_weight = as_column(info[block, 1:2, :])[:, :1]
        paired_weights.append(own_weight + jnp.sum(spread, axis=1, keepdims=True))
    for chunk, arrival in enumerate(arrivals):
        arrival[0].wait()
        for part in range(4):
            scaled = cols_in[chunk, part * lanes : (part + 1) * lanes, :]
            scaled *= columns[:, chunk * 4 + part : chunk * 4 + part + 1]
            at = slice(chunk * count + part * lanes, chunk * count + (part + 1) * lanes)
            au_high[at, :], au_low[at, :] = halves(scaled)
        at = slice(chunk * count, (chunk + 1) * count)
        scaled_cols = (au_high[at, :], au_low[at, :])
        wait_all(arrival[1:])
        for block in range(4):
            rows_at = slice(block * tile, (block + 1) * tile)
            added = products(
                (exps_in[chunk][rows_at, :], exps_in[4 + chunk][rows_at, :]), scaled_cols
            )
            total[rows_at, :] = added if chunk == 0 else total[rows_at, :] + added
    wait_all(last)
    for block in range(4):
        rows_at = slice(block * tile, (block + 1) * tile)
        result = total[rows_at, :] - paired_weights[block] * paired_in[rows_at, :]
        for part in range(4):
            out[part % 2, block, part // 2] = result[part * 64 : (part + 1) * 64]


def losses_kernel(here, there, own_sum, cotangent, scaled, losses):
    mine = pl.ds(pl.multiple_of(lax.axis_index("core") * (quarter + 8), 8), quarter + 8)
    shared = here[mine, :] + there[mine, :]
    own = cotangent[pl.ds(lax.axis_index("yl"), 1), :]
    own = jnp.where(lax.axis_index("core") == 0, own, pltpu.roll(own, 64, 1))
    scaled[...] = as_column(own / own_sum[...])[:quarter, :1] * shared[:quarter, :]
    row = jnp.log(own_sum[...]) - shared[quarter : quarter + 1, :lanes]
    losses[...] = jnp.broadcast_to(row, losses.shape)


def final_kernel(parts, scaled, unit, norms, losses, out):
    del losses
    grad = inv_temp * (jnp.sum(parts[...], axis=0) + scaled[...])
    along = jnp.sum(unit[...] * grad, axis=1, keepdims=True)
    out[...] = (grad - unit[...] * along) / norms[:, :1]


vmem, anywhere = pl.BlockSpec(memory_space=pltpu.VMEM), pl.BlockSpec(memory_space=pl.ANY)


def call(kernel, outs, args, limit, cost=None, scratch=(), far=(), far_outs=()):
    args = [
        pltpu.with_memory_space_constraint(arg, pltpu.HBM) if i in far else arg
        for i, arg in enumerate(args)
    ]
    return pl.pallas_call(
        kernel,
        in_specs=[anywhere if i in far else vmem for i in range(len(args))],
        out_specs=[anywhere if i in far_outs else vmem for i in range(len(outs))],
        out_shape=[
            pltpu.HBM(*out) if i in far_outs else jax.ShapeDtypeStruct(*out)
            for i, out in enumerate(outs)
        ],
        scratch_shapes=list(scratch),
        compiler_params=pltpu.CompilerParams(vmem_limit_bytes=limit * mib),
        cost_estimate=cost,
    )(*args)


def estimate(passes, count, seen, width, exps=0):
    return pl.CostEstimate(
        flops=passes * 2 * count * seen * width,
        bytes_accessed=4 * (count * seen + (count + seen) * width),
        transcendentals=exps,
    )


def passed_along(array, by):
    return lax.ppermute(array, "x", [(i, (i + by) % 4) for i in range(4)])


def per_device(projections, partner, cotangent):
    width = projections.shape[1]
    count, seen = 4 * tile, 8 * quarter
    copies = pltpu.SemaphoreType.DMA
    info = pltpu.VMEM((4, 8, width), f32)
    packed_rows, told, own_unit, norms = call(
        start_kernel,
        [((packed, width), f32), ((8, quarter, width), f32), ((quarter, width), f32),
         ((quarter, lanes), f32)],
        (projections, partner[None], cotangent[None]),
        4,
        scratch=[pltpu.VMEM((1, tile), jnp.int32), pltpu.VMEM((1, tile), f32),
                 pltpu.VMEM((packed, width), f32), copies((3,))],
        far=(0, 1, 2),
        far_outs=(0,),
    )
    here = lax.all_to_all(told, "z", 0, 0, tiled=True).reshape(seen, width)
    rows = lax.all_gather(packed_rows, "yh")
    cols = [here, passed_along(here, 1), passed_along(here, -1), passed_along(here, 2)]
    row_high, row_low, partners = call(
        rows_kernel,
        [((count, width), bf16)] * 2 + [((count, lanes), jnp.int32)],
        (rows,),
        8,
    )
    exps_out = [((count, seen), bf16)] * 2
    row_sums = [((count, width), f32)] * 2
    own_exps = [pltpu.VMEM(*out) for out in exps_out]
    own_rows = [pltpu.VMEM(*out) for out in row_sums]
    highs, lows, col_sums, before = [], [], [], ()
    for chunk in range(2):

        def kernel(*refs, chunk=chunk):
            chunk_kernel(chunk, *refs)

        high, low, sums, *before = call(
            kernel,
            exps_out + [((seen // lanes, lanes), f32), ((count, lanes), f32)] + row_sums[:1],
            (row_high, row_low, cols[chunk], partners, *before),
            24,
            estimate(6, count, seen, width, count * seen),
            own_exps + [copies((4, 2))],
            far_outs=(0, 1),
        )
        highs.append(high)
        lows.append(low)
        col_sums.append(sums)
    hits, plain = before
    high_2, low_2, high_3, low_3, told, shared = call(
        last_kernel,
        exps_out * 2 + [((32, 24, lanes), f32), ((16, quarter + 8, width), f32)],
        (row_high, row_low, *cols[2:], partners, hits, plain, cotangent.reshape(2, lanes), *col_sums),
        32,
        estimate(6, count, 2 * seen, width, 2 * count * seen),
        own_exps * 2
        + [pltpu.VMEM((24, lanes), f32), pltpu.VMEM((32, 24, lanes), f32)]
        + [pltpu.VMEM((16, quarter + 8, width), f32), copies((8, 2)), copies((5, 1))],
        far_outs=range(6),
    )
    highs += [high_2, high_3]
    lows += [low_2, low_3]
    here = lax.psum_scatter(shared.reshape(-1, width), ("yh", "yl"), tiled=True)
    there = lax.ppermute(here, "core", [(0, 1), (1, 0)])
    message = lax.all_to_all(told, ("z", "x"), 0, 0, tiled=True)
    (paired_rows,) = call(
        shadow_kernel,
        row_sums[:1],
        (*cols, rows),
        24,
        estimate(2, count, 4 * seen, width),
        [pltpu.VMEM((4, seen, width), f32), info, own_rows[0], copies((8,))],
        far=range(5),
        far_outs=(0,),
    )
    partial, own_sum = call(
        grad_kernel,
        [((2, 4, 2, quarter, width), f32), ((1, lanes), f32)],
        (message, *highs, *lows, *cols, paired_rows, rows),
        28,
        estimate(3, count, 4 * seen, width),
        own_exps * 4
        + [pltpu.VMEM((4, seen, width), f32), own_rows[0], info]
        + [pltpu.VMEM((16, lanes), f32)] * 2
        + [pltpu.VMEM((4 * seen, width), bf16)] * 2
        + [own_rows[0], copies((6, 4))],
        far=range(1, 15),
    )
    halved = jnp.sum(lax.all_to_all(partial, "core", 0, 0, tiled=True), axis=0)
    swapped = lax.all_to_all(halved.reshape(8, quarter, width), ("yh", "yl"), 0, 0, tiled=True)
    scaled, losses = call(
        losses_kernel,
        [((quarter, width), f32), ((8, lanes), f32)],
        (here, there, own_sum, cotangent.reshape(2, lanes)),
        4,
    )
    losses = lax.all_gather(losses, ("yl", "core"))[:, 0, :quarter].reshape(-1)
    (grads,) = call(
        final_kernel,
        [((quarter, width), f32)],
        (swapped, scaled, own_unit, norms, losses[None]),
        4,
        far=(4,),
    )
    return losses, lax.all_gather(grads, ("yl", "core"), tiled=True)


def solution(mesh):
    fine = Mesh(mesh.devices.reshape(tuple(sizes.values())), tuple(sizes))
    blocks = ("z", "x", "yh")
    return jax.shard_map(
        per_device,
        mesh=fine,
        in_specs=(P(blocks, None), P(blocks), P(blocks)),
        out_specs=(P(blocks), P(blocks, None)),
        check_vma=False,
    )
```
